256 devices in a mesh: expert: 64 (over x_hi, z, y), tensor: 4 (over x_lo, core).
Axes of the slice: x: 4 (x_hi: 2, x_lo: 2; x = x_hi * 2 + x_lo), y: 4, z: 8, core: 2. Of those that a mesh axis runs over, the one named last changes fastest.
Arguments:
- tokens: bfloat16 [16384, 3584], P(('expert', 'tensor')), may hold values from -6 to 6
- expert_ids: int32 [16384, 2], P(('expert', 'tensor')), may hold values from 0 to 63, all different within a row; in each aligned block of 256 rows (0 to 255, 256 to 511, ...) at most 10 rows name the same one
- gate_codes: int32 [16384, 2], P(('expert', 'tensor')), may hold values from 1 to 1023
- dense_up: bfloat16 [3584, 2560], P('expert', 'tensor'), may hold values from -0.09375 to 0.09375
- dense_down: bfloat16 [2560, 3584], P('tensor', 'expert'), may hold values from -0.125 to 0.125
- expert_in: bfloat16 [64, 3584, 2560], P('expert', None, 'tensor'), may hold values from -0.09375 to 0.09375
- expert_out: bfloat16 [64, 2560, 3584], P('expert', 'tensor'), may hold values from -0.125 to 0.125
Outputs:
- layer_out: bfloat16 [16384, 3584], P(('expert', 'tensor'))
The draws below stay inside these ranges and needn't reach their ends.
Inputs may be any that keep to these rules, and one draw needn't show every extreme that they name: `expert_ids`: the two ids of a token differ. In each aligned block of 256 rows no expert is named by more than 10 rows, and in some block one expert is named by exactly 10 rows. Every expert is named somewhere.
All inputs are finite; a program needn't handle non-finite values.
Results may differ from the reference program's by a relative error of at most 0.014.
Values may be sent and summed in bfloat16 or wider, within the bound.
No kernel may reach another device: no remote copies, remote signals or barrier semaphores. Data moves between devices by JAX's collectives and lax.ppermute only.
A program may use at most 192 MiB of HBM per device.

```python
import math
import jax
import jax.numpy as jnp
import numpy as np
from jax import lax

D = 3584
FFE = 2560
DFF = 2560
EXPERTS = 64
GROUP = 256
TOKENS = 16384
CAP = 10
N_TENSOR = 4


def with_ends(array, rng, low, high):
    extent = array.shape
    spot = [jax.random.randint(jax.random.fold_in(rng, axis), (), 0, extent[axis]) for axis in range(len(extent))]
    array = array.at[tuple(spot)].set(low)
    longest = extent.index(max(extent))
    spot[longest] = (spot[longest] + 1) % extent[longest]
    return array.at[tuple(spot)].set(high)


def levels(rng, dims, split, smallest, high):
    def one(axis_at, shards_of):
        draws = jax.random.uniform(jax.random.fold_in(jax.random.fold_in(rng, 6), axis_at), (shards_of,), jnp.float32, smallest / len(split), high / len(split))
        return jnp.repeat(jnp.exp(draws), dims[axis_at] // shards_of).reshape((-1,) + (1,) * (len(dims) - axis_at - 1))

    factor_of = one(*split[0])
    for cut in split[1:]:
        factor_of = factor_of * one(*cut)
    return factor_of


def assign_block(own_key, own, number, rows, amount, top, bound, skew):
    order = jax.random.permutation(own_key, amount)
    crowded, ordinary = portions_of(amount, rows * top, bound, skew, True), portions_of(amount, rows * top, bound, skew, False)
    places = jnp.arange(amount)

    def named(sizes, offset_by):
        used = int((sizes > 0).sum())
        fixed = max(1, used // 4)
        shifted = fixed + (places - fixed + offset_by * (used - fixed)) % max(1, amount - fixed)
        return jnp.zeros((amount,), jnp.int32).at[order[jnp.where(places < fixed, places, shifted)]].set(jnp.asarray(sizes, jnp.int32))

    sizes = jnp.where(number % 4 == 0, named(crowded, number // 4), named(ordinary, number - number // 4 - 1))
    mixed = jax.random.permutation(jax.random.fold_in(own, 3), amount)
    source_of, sink = mixed[0:amount // 2 * 2:2], mixed[1:amount // 2 * 2:2]
    room = jnp.minimum(sizes[source_of] - 1, bound - sizes[sink]) // 2
    room = jnp.where((source_of == order[0]) | (sink == order[0]) | (sizes[sink] == 0), 0, jnp.maximum(room, 0))
    shifted = jax.random.randint(jax.random.fold_in(own, 4), (amount // 2,), 0, 1 << 20) % (room + 1)
    sizes = sizes.at[source_of].add(-shifted).at[sink].add(shifted)
    labels = jnp.searchsorted(jnp.cumsum(sizes), jnp.arange(rows * top), side="right").astype(jnp.int32)
    grid = labels.reshape(top, rows).T
    grid = grid[jax.random.permutation(jax.random.fold_in(own, 1), rows)]
    offset_by = jax.random.randint(jax.random.fold_in(own, 2), (rows, 1), 0, top)
    return jnp.take_along_axis(grid, (jnp.arange(top)[None, :] + offset_by) % top, axis=1)


def portions_of(number_of, total, bound, skew, full):
    portions = [(1 << 20) // math.isqrt(grade ** skew) + 1 for grade in range(1, number_of + 1)]
    largest = bound if full else min(bound, max(-(-total // number_of), total * portions[0] // sum(portions)))
    least = 1 if total - largest >= number_of - 1 else 0
    holding, rest = [largest] + [least] * (number_of - 1), total - largest - least * (number_of - 1)
    while rest > 0:
        free = [i for i in range(1, number_of) if holding[i] < largest] or [i for i in range(1, number_of) if holding[i] < bound]
        whole, budget = sum([portions[i] for i in free]), rest
        for i in free:
            extra = min(bound - holding[i], max(1, budget * portions[i] // whole), rest)
            holding[i] = holding[i] + extra
            rest = rest - extra
    return np.array(holding)


def scatter_about(own_key, dims, scale, most, shards=(), kind=jnp.bfloat16):
    gain = levels(own_key, dims, shards, -0.22, 0.18) if shards else 1.0
    drawn = jax.random.normal(own_key, dims, jnp.float32) * scale * gain
    return jnp.minimum(jnp.maximum(drawn, -most), most).astype(kind)


def setup_inputs(seed: int = 0) -> dict:
    key_of = jax.random.split(jax.random.key(seed), 8)
    tokens = scatter_about(key_of[0], (TOKENS, D), 1.0, 6.0, ((0, 256),))
    expert_ids_keys = jax.random.split(jax.random.fold_in(key_of[1], 1), TOKENS // GROUP)
    expert_ids_turns = jax.random.permutation(jax.random.fold_in(key_of[1], 3), TOKENS // GROUP)
    expert_ids = jax.vmap(lambda own, number: assign_block(jax.random.fold_in(key_of[1], 2), own, number, GROUP, EXPERTS, 2, CAP, 2))(expert_ids_keys, expert_ids_turns).reshape((TOKENS, 2))
    gate_codes = with_ends(jax.random.randint(key_of[2], (TOKENS, 2), 1, 1024), jax.random.fold_in(key_of[2], 1), 1, 1023).astype(jnp.int32)
    dense_up = scatter_about(key_of[3], (D, DFF), D ** -0.5, 0.09375, ((0, 64), (1, 4)))
    dense_down = scatter_about(key_of[4], (DFF, D), DFF ** -0.5, 0.125, ((0, 4), (1, 64)))
    expert_in = scatter_about(key_of[5], (EXPERTS, D, FFE), D ** -0.5, 0.09375, ((0, 64), (2, 4)))
    expert_out = scatter_about(key_of[6], (EXPERTS, FFE, D), FFE ** -0.5, 0.125, ((0, 64), (1, 4)))
    return dict(tokens=tokens, expert_ids=expert_ids, gate_codes=gate_codes, dense_up=dense_up, dense_down=dense_down, expert_in=expert_in, expert_out=expert_out)


def reference(tokens, expert_ids, gate_codes, dense_up, dense_down, expert_in, expert_out):
    f32 = jnp.float32
    groups = TOKENS // GROUP
    pre = jnp.dot(tokens, dense_up, preferred_element_type=f32)
    dense_hidden = jax.nn.silu(pre).astype(jnp.bfloat16)
    dense = jnp.dot(dense_hidden, dense_down, preferred_element_type=f32)

    ids = expert_ids.reshape(groups, 2 * GROUP).astype(jnp.int32)
    onehot = (ids[:, :, None] == jnp.arange(EXPERTS, dtype=jnp.int32)[None, None, :]).astype(jnp.int32)
    before = (jnp.cumsum(onehot, axis=1) - onehot).astype(jnp.int32)
    slot = jnp.sum(before * onehot, axis=2).astype(jnp.int32)
    offsets = (jnp.arange(groups, dtype=jnp.int32) * CAP)[:, None]
    target = (ids * (groups * CAP) + offsets + slot).reshape(-1).astype(jnp.int32)
    source = (jnp.arange(TOKENS * 2, dtype=jnp.int32) // 2).astype(jnp.int32)
    buffer = jnp.zeros((EXPERTS * groups * CAP, D), jnp.bfloat16).at[target].set(tokens[source])
    buffer = buffer.reshape(EXPERTS, groups * CAP, D)
    block = FFE // N_TENSOR

    def serve(item):
        rows_e, w_first, w_second = item
        hidden = jax.nn.silu(jnp.dot(rows_e, w_first, preferred_element_type=f32)).astype(jnp.bfloat16)
        total = jnp.zeros((rows_e.shape[0], D), f32)
        for piece in range(N_TENSOR):
            term = jnp.dot(hidden[:, piece * block:(piece + 1) * block],
                           w_second[piece * block:(piece + 1) * block],
                           preferred_element_type=f32).astype(jnp.bfloat16)
            total = total + lax.optimization_barrier(term).astype(f32)
        return total

    outputs = lax.map(serve, (buffer, expert_in, expert_out))
    picked = outputs.reshape(EXPERTS * groups * CAP, D)[target].reshape(TOKENS, 2, D)
    codes = gate_codes.astype(f32)
    gates = codes / jnp.sum(codes, axis=1, keepdims=True)
    routed = jnp.sum(gates[:, :, None] * picked, axis=1)
    return (tokens.astype(f32) + dense + routed).astype(jnp.bfloat16)
```

```python
import functools

import jax
import jax.numpy as jnp
from jax import lax
from jax.experimental import pallas as pl
from jax.experimental.pallas import tpu as pltpu
from jax.sharding import PartitionSpec as P

F32 = jnp.float32
BF16 = jnp.bfloat16
CORE = [(0, 1), (1, 0), (2, 3), (3, 2)]
NEXT = [(0, 2), (2, 0), (1, 3), (3, 1)]
META = 16
MAIN = 8
VMEM = 48 * 1024 * 1024


def dot(a, b, dims=((1,), (0,))):
    return lax.dot_general(a, b, (dims, ((), ())), preferred_element_type=F32)


def silu(v):
    return v / (1.0 + jnp.exp(-v))


def dispatch_kernel(n_experts, capacity, x_ref, first_ref, second_ref, plan_ref):
    blocks, rows_all, _ = x_ref.shape
    rows = rows_all - META
    group = blocks * rows
    meta = x_ref[0, rows:, :group].astype(F32)
    for b in range(1, blocks):
        meta = meta + x_ref[b, rows:, :group].astype(F32)
    ids = [meta[k : k + 1].astype(jnp.int32) for k in range(2)]
    codes = [meta[2 + k : 3 + k] * 32.0 + meta[4 + k : 5 + k] for k in range(2)]
    names = lax.broadcasted_iota(jnp.int32, (n_experts, group), 0)
    hits = [(names == ids[k]).astype(F32) for k in range(2)]
    earlier = (
        lax.broadcasted_iota(jnp.int32, (group, group), 0)
        < lax.broadcasted_iota(jnp.int32, (group, group), 1)
    )
    before = dot((hits[0] + hits[1]).astype(BF16), earlier.astype(F32).astype(BF16))
    slots = [jnp.sum(hits[k] * before, axis=0, keepdims=True).astype(jnp.int32) for k in range(2)]
    tail = capacity - MAIN
    in_main = [slots[k] < MAIN for k in range(2)]
    spot_main = [ids[k] * MAIN + slots[k] for k in range(2)]
    spot_tail = [ids[k] * tail + slots[k] - MAIN for k in range(2)]
    tokens = jnp.concatenate([x_ref[b, :rows, :] for b in range(blocks)], axis=0)

    def placed(count, spots):
        at = lax.broadcasted_iota(jnp.int32, (count, group), 0)
        hit = jnp.where((at == spots[0]) | (at == spots[1]), 1.0, 0.0)
        return dot(hit.astype(BF16), tokens).astype(BF16)

    first_ref[...] = placed(
        n_experts * MAIN, [jnp.where(in_main[k], spot_main[k], -1) for k in range(2)]
    )
    second_ref[...] = placed(
        n_experts * tail, [jnp.where(in_main[k], -1, spot_tail[k]) for k in range(2)]
    )
    whole = codes[0] + codes[1]
    for k in range(2):
        row = jnp.where(in_main[k], spot_main[k], n_experts * MAIN + spot_tail[k])
        plan_ref[k : k + 1, :] = row.astype(F32)
        plan_ref[2 + k : 3 + k, :] = codes[k] / whole
    plan_ref[4:8, :] = jnp.zeros((4, group), F32)


def dispatch(x, n_experts, capacity):
    blocks, rows_all, width = x.shape
    group = blocks * (rows_all - META)
    return pl.pallas_call(
        functools.partial(dispatch_kernel, n_experts, capacity),
        out_shape=(
            jax.ShapeDtypeStruct((n_experts * MAIN, width), BF16),
            jax.ShapeDtypeStruct((n_experts * (capacity - MAIN), width), BF16),
            jax.ShapeDtypeStruct((8, group), F32),
        ),
        compiler_params=pltpu.CompilerParams(vmem_limit_bytes=VMEM),
        name="dispatch",
    )(x)


def combine_kernel(first_ref, second_ref, plan_ref, out_ref):
    plan = plan_ref[...]
    group = plan.shape[1]
    total = jnp.zeros((group, first_ref.shape[1]), F32)
    start = 0
    for ref in (first_ref, second_ref):
        count = ref.shape[0]
        at = lax.broadcasted_iota(jnp.int32, (count, group), 0) + start
        gate = jnp.zeros((count, group), F32)
        for k in range(2):
            row = plan[k : k + 1].astype(jnp.int32)
            gate = gate + jnp.where(at == row, plan[2 + k : 3 + k], 0.0)
        high = gate.astype(BF16)
        low = (gate - high.astype(F32)).astype(BF16)
        values = ref[...]
        total = total + dot(high, values, ((0,), (0,))) + dot(low, values, ((0,), (0,)))
        start += count
    out_ref[...] = total.astype(BF16)


def combine(first, second, plan):
    return pl.pallas_call(
        combine_kernel,
        out_shape=jax.ShapeDtypeStruct((plan.shape[1], first.shape[1]), BF16),
        compiler_params=pltpu.CompilerParams(vmem_limit_bytes=VMEM),
        name="combine",
    )(first, second, plan)


def block_of(place, step):
    shift = jnp.where(step == 1, 2, jnp.where(step == 2, 1, step))
    return place ^ shift


def experts_kernel(place_ref, x0, x1, x2, x3, up_ref, down_ref, out_ref, pre, hidden):
    step = pl.program_id(0)
    for i, x in enumerate((x0, x1, x2, x3)):

        @pl.when(step == i)
        def _():
            part = dot(x[...], up_ref[...])
            if i == 0:
                pre[...] = part
            elif i < 3:
                pre[...] += part
            else:
                hidden[...] = silu(pre[...] + part).astype(BF16)

    @pl.when(step >= 4)
    def _():
        out_ref[0] = dot(hidden[...], down_ref[...]).astype(BF16)


def experts(place, xs, up, down):
    rows, width = xs[0].shape
    units = up.shape[1]
    whole = pl.BlockSpec((rows, width), lambda i, p: (0, 0))
    return pl.pallas_call(
        experts_kernel,
        grid_spec=pltpu.PrefetchScalarGridSpec(
            num_scalar_prefetch=1,
            grid=(8,),
            in_specs=[whole] * 4
            + [
                pl.BlockSpec((width, units), lambda i, p: (block_of(p[0], jnp.minimum(i, 3)), 0)),
                pl.BlockSpec((units, width), lambda i, p: (0, block_of(p[0], jnp.maximum(i - 4, 0)))),
            ],
            out_specs=pl.BlockSpec((1, rows, width), lambda i, p: (jnp.maximum(i - 4, 0), 0, 0)),
            scratch_shapes=[pltpu.VMEM((rows, units), F32), pltpu.VMEM((rows, units), BF16)],
        ),
        out_shape=jax.ShapeDtypeStruct((4, rows, width), BF16),
        compiler_params=pltpu.CompilerParams(vmem_limit_bytes=VMEM),
        cost_estimate=pl.CostEstimate(
            flops=16 * rows * width * units, bytes_accessed=32 * rows * width, transcendentals=rows * units
        ),
        name="experts",
    )(place, *xs, up, down)


def dense_kernel(parts, x0, x1, x2, x3, up_ref, down_ref, out_ref, pre, hidden):
    step = pl.program_id(0)

    @pl.when(step < parts)
    def _():
        x = jnp.concatenate([x0[...], x1[...], x2[...], x3[...]], axis=0)
        up = up_ref[...].reshape(x.shape[1], up_ref.shape[-1])
        part = dot(x, up)

        @pl.when(step == 0)
        def _():
            pre[...] = part

        @pl.when(step > 0)
        def _():
            pre[...] += part

    @pl.when(step == parts - 1)
    def _():
        hidden[...] = silu(pre[...]).astype(BF16)

    @pl.when(step >= parts)
    def _():
        out = dot(hidden[...], down_ref[...], ((1,), (1,))).astype(BF16)
        out_ref[...] = out.reshape(out_ref.shape)


def dense(xs, up, down):
    rows, width = xs[0].shape
    outer, parts, inner, units = up.shape
    column = outer * inner
    tile = width // 4
    x_spec = pl.BlockSpec((rows, column), lambda i: (0, jnp.minimum(i, parts - 1)))
    return pl.pallas_call(
        functools.partial(dense_kernel, parts),
        grid=(parts + 4,),
        in_specs=[x_spec] * 4
        + [
            pl.BlockSpec((outer, None, inner, units), lambda i: (0, jnp.minimum(i, parts - 1), 0, 0)),
            pl.BlockSpec((tile, units), lambda i: (jnp.maximum(i - parts, 0), 0)),
        ],
        out_specs=pl.BlockSpec((4, rows, tile), lambda i: (0, 0, jnp.maximum(i - parts, 0))),
        out_shape=jax.ShapeDtypeStruct((4, rows, width), BF16),
        scratch_shapes=[pltpu.VMEM((4 * rows, units), F32), pltpu.VMEM((4 * rows, units), BF16)],
        compiler_params=pltpu.CompilerParams(vmem_limit_bytes=VMEM),
        cost_estimate=pl.CostEstimate(
            flops=16 * rows * width * units, bytes_accessed=4 * width * units, transcendentals=4 * rows * units
        ),
        name="dense",
    )(*xs, up, down)


def spread(x):
    other = lax.ppermute(x, "tensor", CORE)
    near = lax.ppermute(x, "tensor", NEXT)
    far = lax.ppermute(near, "tensor", CORE)
    return x, near, other, far


def fold(parts):
    got = lax.ppermute(parts[2:], "tensor", CORE)
    rest = (parts[1].astype(F32) + got[1].astype(F32)).astype(BF16)
    last = lax.ppermute(rest, "tensor", NEXT)
    return parts[0].astype(F32) + got[0].astype(F32), last


N_X, N_Z, N_Y = 2, 8, 4


def expert_at(x, z, y):
    return (x * N_Z + z) * N_Y + y


def lines(axis):
    xs, zs, ys = range(N_X), range(N_Z), range(N_Y)
    if axis == "z":
        return [[expert_at(x, z, y) for z in zs] for x in xs for y in ys]
    return [[expert_at(x, z, y) for y in ys] for x in xs for z in zs]


def gather_dense(dense_up, dense_down):
    index = lax.axis_index("expert")
    rows, units = dense_up.shape
    both = jnp.concatenate([dense_up, dense_down.T], axis=0)
    swap = [(expert_at(x, z, y), expert_at(1 - x, z, y)) for x in range(N_X) for z in range(N_Z) for y in range(N_Y)]
    mate = lax.ppermute(both, "expert", swap)
    low = index < N_Z * N_Y
    pair = jnp.stack([jnp.where(low, both, mate), jnp.where(low, mate, both)])
    up, down = pair[:, :rows], pair[:, rows:]
    turns = [up]
    for shift in range(1, N_Y):
        turns.append(
            lax.ppermute(
                up,
                "expert",
                [
                    (expert_at(x, z, (y + shift) % N_Y), expert_at(x, z, y))
                    for x in range(N_X)
                    for z in range(N_Z)
                    for y in range(N_Y)
                ],
            )
        )
    turns = jnp.stack(turns + turns[:-1])
    start = lax.rem(N_Y - lax.rem(index, N_Y), N_Y)
    up = lax.dynamic_slice_in_dim(turns, start, N_Y, 0)
    up = up.transpose(1, 0, 2, 3).reshape(N_X * N_Y * rows, units)
    up = lax.all_gather(up, "expert", axis=0, tiled=True, axis_index_groups=lines("z"))
    up = up.reshape(N_Z, N_X, N_Y * rows, units)
    down = down.reshape(N_X * rows, units)
    down = lax.all_gather(down, "expert", axis=0, tiled=True, axis_index_groups=lines("z"))
    down = lax.all_gather(down, "expert", axis=0, tiled=True, axis_index_groups=lines("y"))
    down = down.reshape(N_Y, N_Z, N_X, rows, units).transpose(2, 1, 0, 3, 4).reshape(-1, units)
    return up, down


def local(tokens, expert_ids, gate_codes, dense_up, dense_down, expert_in, expert_out):
    rows_own, width = tokens.shape
    place = lax.axis_index("tensor")
    n_tensor = lax.axis_size("tensor")
    group = rows_own * n_tensor
    n_experts = lax.axis_size("expert") * expert_in.shape[0]
    capacity = 5 * group // (2 * n_experts)
    part = width // n_tensor

    ids, codes = expert_ids.astype(jnp.int32).T, gate_codes.astype(jnp.int32).T
    meta = jnp.concatenate([ids, codes // 32, codes % 32, jnp.zeros((META - 6, rows_own), jnp.int32)])
    owner = jnp.arange(group, dtype=jnp.int32)[None, :] // rows_own
    meta = jnp.where(owner == place, jnp.tile(meta, (1, n_tensor)), 0).astype(BF16)
    meta = jnp.pad(meta, ((0, 0), (0, part - group)))
    columns = tokens.reshape(rows_own, n_tensor, part).transpose(1, 0, 2)
    sent = jnp.concatenate([columns, jnp.broadcast_to(meta, (n_tensor,) + meta.shape)], axis=1)
    grouped = lax.all_to_all(sent, "tensor", split_axis=0, concat_axis=0, tiled=True)

    up_all, down_all = gather_dense(dense_up, dense_down)

    first, second, plan = dispatch(grouped, n_experts, capacity)
    first = lax.all_to_all(
        first.reshape(n_experts, MAIN, part), "expert", split_axis=0, concat_axis=0, tiled=True
    )
    second = lax.all_to_all(
        second.reshape(n_experts, capacity - MAIN, part), "expert", split_axis=0, concat_axis=0, tiled=True
    )
    received = jnp.concatenate([first.reshape(-1, part), second.reshape(-1, part)], axis=0)
    result = experts(place.reshape(1), spread(received), expert_in[0], expert_out[0])
    term, last = fold(result)
    result = (term + last.astype(F32)).astype(BF16)
    cut = n_experts * MAIN
    first = lax.all_to_all(
        result[:cut].reshape(n_experts, MAIN, part), "expert", split_axis=0, concat_axis=0, tiled=True
    )
    second = lax.all_to_all(
        result[cut:].reshape(n_experts, capacity - MAIN, part), "expert", split_axis=0, concat_axis=0, tiled=True
    )
    routed = combine(first.reshape(-1, part), second.reshape(-1, part), plan)

    dense_parts = dense(spread(tokens), up_all, down_all)
    dense_term, dense_last = fold(dense_parts)

    routed = lax.all_to_all(
        routed.reshape(n_tensor, rows_own, part), "tensor", split_axis=0, concat_axis=0, tiled=True
    )
    routed = routed.transpose(1, 0, 2).reshape(rows_own, width)
    total = tokens.astype(F32) + dense_term + dense_last.astype(F32) + routed.astype(F32)
    return total.astype(BF16)


def solution(mesh):
    return jax.shard_map(
        local,
        mesh=mesh,
        in_specs=(
            P(("expert", "tensor"), None),
            P(("expert", "tensor"), None),
            P(("expert", "tensor"), None),
            P("expert", "tensor"),
            P("tensor", "expert"),
            P("expert", None, "tensor"),
            P("expert", "tensor", None),
        ),
        out_specs=P(("expert", "tensor"), None),
        check_vma=False,
    )
```

```python
import functools

import jax
import jax.numpy as jnp
from jax import lax
from jax.experimental import pallas as pl
from jax.experimental.pallas import tpu as pltpu
from jax.sharding import PartitionSpec as P

F32 = jnp.float32
BF16 = jnp.bfloat16
CORE = [(0, 1), (1, 0), (2, 3), (3, 2)]
NEXT = [(0, 2), (2, 0), (1, 3), (3, 1)]
FAR = [(0, 3), (3, 0), (1, 2), (2, 1)]
N_X, N_Z, N_Y = 2, 8, 4
META = 16
MAIN = 8
LANES = 128
HALVES = 2
VMEM = 32 * 1024 * 1024


def dot(a, b, dims=((1,), (0,))):
    return lax.dot_general(a, b, (dims, ((), ())), preferred_element_type=F32)


def silu(v):
    return v / (1.0 + jnp.exp(-v))


def flip(step):
    return (0, 2, 1, 3)[step]


def at(place, step, size):
    return pl.multiple_of((place ^ flip(step)) * size, size)


def tiles_of(width, capacity):
    return width // LANES + capacity - MAIN


def put_tiles(ref, lead, scratch, main, tail, count, capacity):
    n, extra = main.shape[1] // LANES, capacity - MAIN
    for j in range(n):
        piece = main[:, j * LANES : (j + 1) * LANES].reshape(count, MAIN, LANES)
        ref[lead + (slice(None), j)] = piece.astype(BF16)
    for s in range(extra):
        for j in range(n):
            rows = pl.ds(s * MAIN + j, count, stride=extra * MAIN)
            scratch[rows, :] = tail[s * count : (s + 1) * count, j * LANES : (j + 1) * LANES]
    rest = scratch[...].reshape(count, extra, MAIN, LANES)
    for s in range(extra):
        ref[lead + (slice(None), n + s)] = rest[:, s].astype(BF16)


def take_tiles(ref, scratch, count, capacity):
    extra = capacity - MAIN
    n = ref.shape[1] - extra
    main = [
        ref[:, j].astype(F32).reshape(count * MAIN, LANES).astype(BF16) for j in range(n)
    ]
    scratch[...] = ref[:, n:].astype(F32).reshape(count * extra * MAIN, LANES)
    tail = []
    for s in range(extra):
        cut = [scratch[pl.ds(s * MAIN + j, count, stride=extra * MAIN), :] for j in range(n)]
        tail.append(jnp.concatenate(cut, axis=1).astype(BF16))
    return jnp.concatenate([jnp.concatenate(main, axis=1)] + tail, axis=0)


def clear(scratch):
    scratch[...] = jnp.zeros(scratch.shape, scratch.dtype)


SMEM = pl.BlockSpec(memory_space=pltpu.SMEM)
WHOLE = pl.BlockSpec(memory_space=pltpu.VMEM)
PARAMS = pltpu.CompilerParams(vmem_limit_bytes=VMEM)


def pack_kernel(place_ref, tokens_ref, meta_ref, *out_refs):
    rows, part = tokens_ref.shape[0], out_refs[0].shape[1]
    for step, out_ref in enumerate(out_refs):
        out_ref[:rows, :] = tokens_ref[:, pl.ds(at(place_ref[0], step, part), part)]
        out_ref[rows:, :] = meta_ref[...]


def pack(place, tokens, meta):
    rows, width = tokens.shape
    block = jax.ShapeDtypeStruct((rows + META, width // 4), BF16)
    return pl.pallas_call(
        pack_kernel,
        in_specs=[SMEM, WHOLE, WHOLE],
        out_specs=[WHOLE] * 4,
        out_shape=[block] * 4,
        compiler_params=PARAMS,
        name="pack",
    )(place, tokens, meta)


def dispatch_kernel(n_experts, capacity, place_ref, x0, x1, x2, x3, out_ref, plan_ref, tokens, scratch):
    rows = x0.shape[0] - META
    group = 4 * rows
    meta = jnp.zeros((META, group), F32)
    for step, x in enumerate((x0, x1, x2, x3)):
        meta = meta + x[rows:, :group].astype(F32)
        tokens[pl.ds(at(place_ref[0], step, rows), rows), :] = x[:rows, :]
    ids = [meta[k : k + 1].astype(jnp.int32) for k in range(2)]
    codes = [meta[2 + k : 3 + k] * 32.0 + meta[4 + k : 5 + k] for k in range(2)]
    names = lax.broadcasted_iota(jnp.int32, (n_experts, group), 0)
    hits = [(names == ids[k]).astype(F32) for k in range(2)]
    earlier = (
        lax.broadcasted_iota(jnp.int32, (group, group), 0)
        < lax.broadcasted_iota(jnp.int32, (group, group), 1)
    )
    before = dot((hits[0] + hits[1]).astype(BF16), earlier.astype(F32).astype(BF16))
    slots = [jnp.sum(hits[k] * before, axis=0, keepdims=True).astype(jnp.int32) for k in range(2)]
    in_main = [slots[k] < MAIN for k in range(2)]
    spot_main = [ids[k] * MAIN + slots[k] for k in range(2)]
    spot_tail = [(slots[k] - MAIN) * n_experts + ids[k] for k in range(2)]

    def placed(count, spots):
        row = lax.broadcasted_iota(jnp.int32, (count, group), 0)
        hit = jnp.where((row == spots[0]) | (row == spots[1]), 1.0, 0.0)
        return dot(hit.astype(BF16), tokens[...])

    main = placed(n_experts * MAIN, [jnp.where(in_main[k], spot_main[k], -1) for k in range(2)])
    tail = placed(
        n_experts * (capacity - MAIN), [jnp.where(in_main[k], -1, spot_tail[k]) for k in range(2)]
    )
    clear(scratch)
    put_tiles(out_ref, (), scratch, main, tail, n_experts, capacity)
    whole = codes[0] + codes[1]
    for k in range(2):
        row = jnp.where(in_main[k], spot_main[k], n_experts * MAIN + spot_tail[k])
        plan_ref[k : k + 1, :] = row.astype(F32)
        plan_ref[2 + k : 3 + k, :] = codes[k] / whole
    plan_ref[4:8, :] = jnp.zeros((4, group), F32)


def dispatch(place, xs, n_experts, capacity):
    rows_all, width = xs[0].shape
    group = 4 * (rows_all - META)
    return pl.pallas_call(
        functools.partial(dispatch_kernel, n_experts, capacity),
        in_specs=[SMEM] + [WHOLE] * 4,
        out_specs=[WHOLE] * 2,
        out_shape=[
            jax.ShapeDtypeStruct((n_experts, tiles_of(width, capacity), MAIN, LANES), BF16),
            jax.ShapeDtypeStruct((8, group), F32),
        ],
        scratch_shapes=[
            pltpu.VMEM((group, width), BF16),
            pltpu.VMEM((n_experts * (capacity - MAIN) * MAIN, LANES), F32),
        ],
        compiler_params=PARAMS,
        name="dispatch",
    )(place, *xs)


def experts_kernel(capacity, place_ref, x0, x1, x2, x3, up_ref, down_ref, mine_ref, others_ref, x_all, scratch):
    count, tiles = x0.shape[:2]
    width = (tiles - capacity + MAIN) * LANES
    for step, x in enumerate((x0, x1, x2, x3)):
        x_all[:, pl.ds(at(place_ref[0], step, width), width)] = take_tiles(x, scratch, count, capacity)
    hidden = silu(dot(x_all[...], up_ref[...])).astype(BF16)
    clear(scratch)
    for step in (2, 3, 0, 1):
        out = dot(hidden, down_ref[:, pl.ds(at(place_ref[0], step, width), width)])
        ref = mine_ref if step < 2 else others_ref
        put_tiles(ref, (step % 2,), scratch, out[: count * MAIN], out[count * MAIN :], count, capacity)


def experts(place, xs, up, down, capacity):
    count, tiles = xs[0].shape[:2]
    width, units = up.shape
    rows = count * capacity
    pair = jax.ShapeDtypeStruct((2,) + xs[0].shape, BF16)
    return pl.pallas_call(
        functools.partial(experts_kernel, capacity),
        in_specs=[SMEM] + [WHOLE] * 6,
        out_specs=[WHOLE] * 2,
        out_shape=[pair] * 2,
        scratch_shapes=[
            pltpu.VMEM((rows, width), BF16),
            pltpu.VMEM((count * (capacity - MAIN) * MAIN, LANES), F32),
        ],
        compiler_params=PARAMS,
        cost_estimate=pl.CostEstimate(
            flops=4 * rows * width * units,
            bytes_accessed=4 * width * (rows + units),
            transcendentals=rows * units,
        ),
        name="experts",
    )(place, *xs, up, down)


def combine_kernel(capacity, place_ref, x_ref, plan_ref, o0, o1, o2, o3, scratch, routed):
    count = x_ref.shape[0]
    plan = plan_ref[...]
    group = plan.shape[1]
    values = take_tiles(x_ref, scratch, count, capacity)
    row = lax.broadcasted_iota(jnp.int32, (count * capacity, group), 0)
    gate = jnp.zeros((count * capacity, group), F32)
    for k in range(2):
        gate = gate + jnp.where(row == plan[k : k + 1].astype(jnp.int32), plan[2 + k : 3 + k], 0.0)
    high = gate.astype(BF16)
    low = (gate - high.astype(F32)).astype(BF16)
    routed[...] = (dot(high, values, ((0,), (0,))) + dot(low, values, ((0,), (0,)))).astype(BF16)
    for step, ref in enumerate((o0, o1, o2, o3)):
        ref[...] = routed[pl.ds(at(place_ref[0], step, group // 4), group // 4), :]


def combine(place, x, plan, capacity):
    count, tiles = x.shape[:2]
    width = (tiles - capacity + MAIN) * LANES
    group = plan.shape[1]
    return pl.pallas_call(
        functools.partial(combine_kernel, capacity),
        in_specs=[SMEM] + [WHOLE] * 2,
        out_specs=[WHOLE] * 4,
        out_shape=[jax.ShapeDtypeStruct((group // 4, width), BF16)] * 4,
        scratch_shapes=[
            pltpu.VMEM((count * (capacity - MAIN) * MAIN, LANES), F32),
            pltpu.VMEM((group, width), BF16),
        ],
        compiler_params=PARAMS,
        name="combine",
    )(place, x, plan)


def dense_kernel(x0, x1, x2, x3, up_ref, down_ref, mine_ref, others_ref, pre, hidden):
    step = pl.program_id(0)

    @pl.when(step < N_X)
    def _():
        x = jnp.concatenate([x0[...], x1[...], x2[...], x3[...]], axis=0)
        up = up_ref[...].astype(F32).reshape(x.shape[1], up_ref.shape[-1]).astype(BF16)
        part = dot(x, up)

        @pl.when(step == 0)
        def _():
            pre[...] = part

        @pl.when(step > 0)
        def _():
            hidden[...] = silu(pre[...] + part).astype(BF16)

    @pl.when(step >= N_X)
    def _():
        down = down_ref[...].astype(F32)
        down = down.reshape(-1, down.shape[-1]).astype(BF16)
        out = dot(hidden[...], down, ((1,), (1,))).astype(BF16).reshape((4,) + mine_ref.shape[1:])
        mine_ref[...] = out[:2]
        others_ref[...] = out[2:]


def dense(xs, weights):
    rows, width = xs[0].shape
    units = weights.shape[-1]
    z, y, _, _, inner, _ = weights.shape
    tile = width // 4
    x_spec = pl.BlockSpec((rows, width // N_X), lambda i: (0, jnp.minimum(i, N_X - 1)))
    out_spec = pl.BlockSpec((2, rows, tile), lambda i: (0, 0, jnp.maximum(i - N_X, 0)))

    def down_at(i):
        n = jnp.maximum(i - N_X, 0)
        return n % 2, 0, n // 2, 1, 0, 0

    return pl.pallas_call(
        dense_kernel,
        grid=(N_X + 4,),
        in_specs=[x_spec] * 4
        + [
            pl.BlockSpec((z, y, None, None, inner, units), lambda i: (0, 0, jnp.minimum(i, N_X - 1), 0, 0, 0)),
            pl.BlockSpec((z // 2, y, None, None, inner, units), down_at),
        ],
        out_specs=[out_spec] * 2,
        out_shape=[jax.ShapeDtypeStruct((2, rows, width), BF16)] * 2,
        scratch_shapes=[pltpu.VMEM((4 * rows, units), F32), pltpu.VMEM((4 * rows, units), BF16)],
        compiler_params=PARAMS,
        cost_estimate=pl.CostEstimate(
            flops=16 * rows * width * units, bytes_accessed=4 * width * units, transcendentals=4 * rows * units
        ),
        name="dense",
    )(*xs, weights, weights)


def finish_kernel(place_ref, tokens_ref, mine_ref, got_ref, last_ref, r0, r1, r2, r3, out_ref):
    part = r0.shape[1]
    for step, ref in enumerate((r0, r1, r2, r3)):
        columns = pl.ds(at(place_ref[0], step, part), part)
        total = tokens_ref[:, columns].astype(F32) + mine_ref[0, :, columns].astype(F32)
        total = total + got_ref[0, :, columns].astype(F32) + last_ref[:, columns].astype(F32)
        out_ref[:, columns] = (total + ref[...].astype(F32)).astype(BF16)


def finish(place, tokens, mine, got, last, routed):
    return pl.pallas_call(
        finish_kernel,
        in_specs=[SMEM] + [WHOLE] * 8,
        out_specs=WHOLE,
        out_shape=jax.ShapeDtypeStruct(tokens.shape, BF16),
        compiler_params=PARAMS,
        name="finish",
    )(place, tokens, mine, got, last, *routed)


def swap(xs):
    return [xs[0]] + [lax.ppermute(x, "tensor", perm) for x, perm in zip(xs[1:], (NEXT, CORE, FAR))]


def spread(x, near):
    other = lax.ppermute(x, "tensor", CORE)
    far = lax.ppermute(near, "tensor", CORE)
    return x, near, other, far


def fold(mine, others):
    got = lax.ppermute(others, "tensor", CORE)
    rest = (mine[1].astype(F32) + got[1].astype(F32)).astype(BF16)
    return got, lax.ppermute(rest, "tensor", NEXT)


def expert_at(x, z, y):
    return (x * N_Z + z) * N_Y + y


def gather_dense(dense_up, dense_down, after):
    rows, units = dense_up.shape
    places = [(x, z, y) for x in range(N_X) for z in range(N_Z) for y in range(N_Y)]
    both = jnp.concatenate([dense_up, dense_down.T], axis=0)
    mate = lax.ppermute(both, "expert", [(expert_at(x, z, y), expert_at(1 - x, z, y)) for x, z, y in places])
    mate, after = lax.optimization_barrier((mate, after))
    low = lax.axis_index("expert") < N_Z * N_Y
    pair = jnp.concatenate([jnp.where(low, both, mate), jnp.where(low, mate, both)])
    planes = [[expert_at(x, z, y) for z in range(N_Z) for y in range(N_Y)] for x in range(N_X)]
    out = lax.all_gather(pair, "expert", axis=0, tiled=True, axis_index_groups=planes)
    return out.reshape(N_Z, N_Y, N_X, 2, rows, units), after


def local(tokens, expert_ids, gate_codes, dense_up, dense_down, expert_in, expert_out):
    rows_own, width = tokens.shape
    place = lax.axis_index("tensor")
    spot = place.reshape(1)
    n_tensor = lax.axis_size("tensor")
    group = rows_own * n_tensor
    n_experts = lax.axis_size("expert") * expert_in.shape[0]
    capacity = 5 * group // (2 * n_experts)
    part = width // n_tensor

    ids, codes = expert_ids.astype(jnp.int32).T, gate_codes.astype(jnp.int32).T
    meta = jnp.concatenate([ids, codes // 32, codes % 32, jnp.zeros((META - 6, rows_own), jnp.int32)])
    owner = jnp.arange(group, dtype=jnp.int32)[None, :] // rows_own
    meta = jnp.where(owner == place, jnp.tile(meta, (1, n_tensor)), 0).astype(BF16)
    meta = jnp.pad(meta, ((0, 0), (0, part - group)))
    grouped = swap(pack(spot, tokens, meta))
    weights, grouped = gather_dense(dense_up, dense_down, grouped)
    routed, plan = dispatch(spot, grouped, n_experts, capacity)

    routed = lax.all_to_all(routed, "expert", split_axis=0, concat_axis=0, tiled=True)
    size = n_experts // HALVES
    results, near = [], None
    for half in range(HALVES):
        x = routed[half * size : (half + 1) * size]
        if near is not None:
            x, near = lax.optimization_barrier((x, near))
        near = lax.ppermute(x, "tensor", NEXT)
        mine, others = experts(spot, spread(x, near), expert_in[0], expert_out[0], capacity)
        got, last = fold(mine, others)
        results.append((mine[0].astype(F32) + got[0].astype(F32) + last.astype(F32)).astype(BF16))
    result = jnp.concatenate(results)

    dense_own, result = lax.optimization_barrier((tokens, result))
    blocks = spread(tokens, lax.ppermute(tokens, "tensor", NEXT))
    mine, others = dense((dense_own,) + blocks[1:], weights)
    got, last = fold(mine, others)

    returned = lax.all_to_all(result, "expert", split_axis=0, concat_axis=0, tiled=True)
    pieces = swap(combine(spot, returned, plan, capacity))
    return finish(spot, tokens, mine, got, last, pieces)


def solution(mesh):
    return jax.shard_map(
        local,
        mesh=mesh,
        in_specs=(
            P(("expert", "tensor"), None),
            P(("expert", "tensor"), None),
            P(("expert", "tensor"), None),
            P("expert", "tensor"),
            P("tensor", "expert"),
            P("expert", None, "tensor"),
            P("expert", "tensor", None),
        ),
        out_specs=P(("expert", "tensor"), None),
        check_vma=False,
    )
```

```python
import functools

import jax
import jax.numpy as jnp
from jax import lax
from jax.experimental import pallas as pl
from jax.experimental.pallas import tpu as pltpu
from jax.sharding import PartitionSpec as P

F32 = jnp.float32
BF16 = jnp.bfloat16
CORE = [(0, 1), (1, 0), (2, 3), (3, 2)]
NEXT = [(0, 2), (2, 0), (1, 3), (3, 1)]
FAR = [(0, 3), (3, 0), (1, 2), (2, 1)]
N_X, N_Z, N_Y = 2, 8, 4
META = 16
MAIN = 8
LANES = 128
SIZES = (32, 32)
VMEM = 24 * 1024 * 1024


def dot(a, b, dims=((1,), (0,))):
    return lax.dot_general(a, b, (dims, ((), ())), preferred_element_type=F32)


def silu(v):
    return v / (1.0 + jnp.exp(-v))


def flip(step):
    return (0, 2, 1, 3)[step]


def at(place, step, size):
    return pl.multiple_of((place ^ flip(step)) * size, size)


def tiles_of(width, capacity):
    return width // LANES + capacity - MAIN


def put_tiles(ref, lead, scratch, main, tail, count, capacity):
    n, extra = main.shape[1] // LANES, capacity - MAIN
    for j in range(n):
        piece = main[:, j * LANES : (j + 1) * LANES].reshape(count, MAIN, LANES)
        ref[lead + (slice(None), j)] = piece.astype(BF16)
    for s in range(extra):
        for j in range(n):
            rows = pl.ds(s * MAIN + j, count, stride=extra * MAIN)
            scratch[rows, :] = tail[s * count : (s + 1) * count, j * LANES : (j + 1) * LANES]
    rest = scratch[...].reshape(count, extra, MAIN, LANES)
    for s in range(extra):
        ref[lead + (slice(None), n + s)] = rest[:, s].astype(BF16)


def take_tiles(ref, scratch, count, capacity):
    extra = capacity - MAIN
    n = ref.shape[1] - extra
    main = [ref[:, j].astype(F32).reshape(count * MAIN, LANES) for j in range(n)]
    scratch[...] = ref[:, n:].astype(F32).reshape(count * extra * MAIN, LANES)
    tail = []
    for s in range(extra):
        cut = [scratch[pl.ds(s * MAIN + j, count, stride=extra * MAIN), :] for j in range(n)]
        tail.append(jnp.concatenate(cut, axis=1))
    return jnp.concatenate([jnp.concatenate(main, axis=1)] + tail, axis=0).astype(BF16)


def clear(scratch):
    scratch[...] = jnp.zeros(scratch.shape, scratch.dtype)


SMEM = pl.BlockSpec(memory_space=pltpu.SMEM)
WHOLE = pl.BlockSpec(memory_space=pltpu.VMEM)
COST = pl.CostEstimate(flops=1, bytes_accessed=1, transcendentals=0)
PARAMS = pltpu.CompilerParams(vmem_limit_bytes=VMEM)


def pack_kernel(place_ref, tokens_ref, meta_ref, *out_refs):
    rows, part = tokens_ref.shape[0], out_refs[0].shape[1]
    for step, out_ref in enumerate(out_refs):
        out_ref[:rows, :] = tokens_ref[:, pl.ds(at(place_ref[0], step, part), part)]
        out_ref[rows:, :] = meta_ref[...]


def pack(place, tokens, meta):
    rows, width = tokens.shape
    block = jax.ShapeDtypeStruct((rows + META, width // 4), BF16)
    return pl.pallas_call(
        pack_kernel,
        in_specs=[SMEM, WHOLE, WHOLE],
        out_specs=[WHOLE] * 4,
        out_shape=[block] * 4,
        compiler_params=PARAMS,
        cost_estimate=COST,
        name="pack",
    )(place, tokens, meta)


def dispatch_kernel(n_experts, capacity, place_ref, x0, x1, x2, x3, out_ref, plan_ref, tokens, scratch):
    rows = x0.shape[0] - META
    group = 4 * rows
    meta = jnp.zeros((META, group), F32)
    for step, x in enumerate((x0, x1, x2, x3)):
        meta = meta + x[rows:, :group].astype(F32)
        tokens[pl.ds(at(place_ref[0], step, rows), rows), :] = x[:rows, :]
    ids = [meta[k : k + 1].astype(jnp.int32) for k in range(2)]
    codes = [meta[2 + k : 3 + k] * 32.0 + meta[4 + k : 5 + k] for k in range(2)]
    names = lax.broadcasted_iota(jnp.int32, (n_experts, group), 0)
    hits = [(names == ids[k]).astype(F32) for k in range(2)]
    earlier = (
        lax.broadcasted_iota(jnp.int32, (group, group), 0)
        < lax.broadcasted_iota(jnp.int32, (group, group), 1)
    )
    before = dot((hits[0] + hits[1]).astype(BF16), earlier.astype(F32).astype(BF16))
    slots = [jnp.sum(hits[k] * before, axis=0, keepdims=True).astype(jnp.int32) for k in range(2)]
    in_main = [slots[k] < MAIN for k in range(2)]
    spot_main = [ids[k] * MAIN + slots[k] for k in range(2)]
    spot_tail = [(slots[k] - MAIN) * n_experts + ids[k] for k in range(2)]

    def placed(count, spots):
        row = lax.broadcasted_iota(jnp.int32, (count, group), 0)
        hit = jnp.where((row == spots[0]) | (row == spots[1]), 1.0, 0.0)
        return dot(hit.astype(BF16), tokens[...])

    main = placed(n_experts * MAIN, [jnp.where(in_main[k], spot_main[k], -1) for k in range(2)])
    tail = placed(
        n_experts * (capacity - MAIN), [jnp.where(in_main[k], -1, spot_tail[k]) for k in range(2)]
    )
    clear(scratch)
    put_tiles(out_ref, (), scratch, main, tail, n_experts, capacity)
    whole = codes[0] + codes[1]
    for k in range(2):
        row = jnp.where(in_main[k], spot_main[k], n_experts * MAIN + spot_tail[k])
        plan_ref[k : k + 1, :] = row.astype(F32)
        plan_ref[2 + k : 3 + k, :] = codes[k] / whole
    plan_ref[4:8, :] = jnp.zeros((4, group), F32)


def dispatch(place, xs, n_experts, capacity):
    rows_all, width = xs[0].shape
    group = 4 * (rows_all - META)
    return pl.pallas_call(
        functools.partial(dispatch_kernel, n_experts, capacity),
        in_specs=[SMEM] + [WHOLE] * 4,
        out_specs=[WHOLE] * 2,
        out_shape=[
            jax.ShapeDtypeStruct((n_experts, tiles_of(width, capacity), MAIN, LANES), BF16),
            jax.ShapeDtypeStruct((8, group), F32),
        ],
        scratch_shapes=[
            pltpu.VMEM((group, width), BF16),
            pltpu.VMEM((n_experts * (capacity - MAIN) * MAIN, LANES), F32),
        ],
        compiler_params=PARAMS,
        cost_estimate=COST,
        name="dispatch",
    )(place, *xs)


def experts_kernel(capacity, place_ref, x0, x1, x2, x3, up_ref, down_ref, o0, o1, o2, o3, x_all, scratch):
    count, tiles = x0.shape[:2]
    width = (tiles - capacity + MAIN) * LANES
    for step, x in enumerate((x0, x1, x2, x3)):
        x_all[:, pl.ds(at(place_ref[0], step, width), width)] = take_tiles(x, scratch, count, capacity)
    hidden = silu(dot(x_all[...], up_ref[...])).astype(BF16)
    clear(scratch)
    for step, ref in enumerate((o0, o1, o2, o3)):
        out = dot(hidden, down_ref[:, pl.ds(at(place_ref[0], step, width), width)])
        put_tiles(ref, (), scratch, out[: count * MAIN], out[count * MAIN :], count, capacity)


def experts(place, xs, up, down, capacity):
    count, tiles = xs[0].shape[:2]
    width, units = up.shape
    rows = count * capacity
    return pl.pallas_call(
        functools.partial(experts_kernel, capacity),
        in_specs=[SMEM] + [WHOLE] * 6,
        out_specs=[WHOLE] * 4,
        out_shape=[jax.ShapeDtypeStruct(xs[0].shape, BF16)] * 4,
        scratch_shapes=[
            pltpu.VMEM((rows, width), BF16),
            pltpu.VMEM((count * (capacity - MAIN) * MAIN, LANES), F32),
        ],
        compiler_params=PARAMS,
        cost_estimate=COST,
        name="experts",
    )(place, *xs, up, down)


def combine_kernel(capacity, place_ref, x_ref, plan_ref, o0, o1, o2, o3, scratch, routed):
    count = x_ref.shape[0]
    plan = plan_ref[...]
    group = plan.shape[1]
    values = take_tiles(x_ref, scratch, count, capacity)
    row = lax.broadcasted_iota(jnp.int32, (count * capacity, group), 0)
    gate = jnp.zeros((count * capacity, group), F32)
    for k in range(2):
        gate = gate + jnp.where(row == plan[k : k + 1].astype(jnp.int32), plan[2 + k : 3 + k], 0.0)
    high = gate.astype(BF16)
    low = (gate - high.astype(F32)).astype(BF16)
    routed[...] = (dot(high, values, ((0,), (0,))) + dot(low, values, ((0,), (0,)))).astype(BF16)
    for step, ref in enumerate((o0, o1, o2, o3)):
        ref[...] = routed[pl.ds(at(place_ref[0], step, group // 4), group // 4), :]


def combine(place, x, plan, capacity):
    count, tiles = x.shape[:2]
    width = (tiles - capacity + MAIN) * LANES
    group = plan.shape[1]
    return pl.pallas_call(
        functools.partial(combine_kernel, capacity),
        in_specs=[SMEM] + [WHOLE] * 2,
        out_specs=[WHOLE] * 4,
        out_shape=[jax.ShapeDtypeStruct((group // 4, width), BF16)] * 4,
        scratch_shapes=[
            pltpu.VMEM((count * (capacity - MAIN) * MAIN, LANES), F32),
            pltpu.VMEM((group, width), BF16),
        ],
        compiler_params=PARAMS,
        cost_estimate=COST,
        name="combine",
    )(place, x, plan)


def dense_kernel(x0, x1, x2, x3, up_ref, down_ref, mine_ref, others_ref, pre, hidden):
    step = pl.program_id(0)

    @pl.when(step < N_X)
    def _():
        x = jnp.concatenate([x0[...], x1[...], x2[...], x3[...]], axis=0)
        up = up_ref[...].astype(F32).reshape(x.shape[1], up_ref.shape[-1]).astype(BF16)
        part = dot(x, up)

        @pl.when(step == 0)
        def _():
            pre[...] = part

        @pl.when(step > 0)
        def _():
            hidden[...] = silu(pre[...] + part).astype(BF16)

    @pl.when(step >= N_X)
    def _():
        down = down_ref[...].astype(F32)
        down = down.reshape(-1, down.shape[-1]).astype(BF16)
        out = dot(hidden[...], down, ((1,), (1,))).astype(BF16).reshape((4,) + mine_ref.shape[1:])
        mine_ref[...] = out[:2]
        others_ref[...] = out[2:]


def dense(xs, weights):
    rows, width = xs[0].shape
    units = weights.shape[-1]
    z, y, _, _, inner, _ = weights.shape
    tile = width // 4
    x_spec = pl.BlockSpec((rows, width // N_X), lambda i: (0, jnp.minimum(i, N_X - 1)))
    out_spec = pl.BlockSpec((2, rows, tile), lambda i: (0, 0, jnp.maximum(i - N_X, 0)))

    def down_at(i):
        n = jnp.maximum(i - N_X, 0)
        return n % 2, 0, n // 2, 1, 0, 0

    return pl.pallas_call(
        dense_kernel,
        grid=(N_X + 4,),
        in_specs=[x_spec] * 4
        + [
            pl.BlockSpec((z, y, None, None, inner, units), lambda i: (0, 0, jnp.minimum(i, N_X - 1), 0, 0, 0)),
            pl.BlockSpec((z // 2, y, None, None, inner, units), down_at),
        ],
        out_specs=[out_spec] * 2,
        out_shape=[jax.ShapeDtypeStruct((2, rows, width), BF16)] * 2,
        scratch_shapes=[pltpu.VMEM((4 * rows, units), F32), pltpu.VMEM((4 * rows, units), BF16)],
        compiler_params=PARAMS,
        cost_estimate=COST,
        name="dense",
    )(*xs, weights, weights)


def finish_kernel(place_ref, tokens_ref, mine_ref, got_ref, last_ref, r0, r1, r2, r3, out_ref):
    part = r0.shape[1]
    for step, ref in enumerate((r0, r1, r2, r3)):
        columns = pl.ds(at(place_ref[0], step, part), part)
        total = tokens_ref[:, columns].astype(F32) + mine_ref[0, :, columns].astype(F32)
        total = total + got_ref[0, :, columns].astype(F32) + last_ref[:, columns].astype(F32)
        out_ref[:, columns] = (total + ref[...].astype(F32)).astype(BF16)


def finish(place, tokens, mine, got, last, routed):
    return pl.pallas_call(
        finish_kernel,
        in_specs=[SMEM] + [WHOLE] * 8,
        out_specs=WHOLE,
        out_shape=jax.ShapeDtypeStruct(tokens.shape, BF16),
        compiler_params=PARAMS,
        cost_estimate=COST,
        name="finish",
    )(place, tokens, mine, got, last, *routed)


def swap(xs):
    return [xs[0]] + [lax.ppermute(x, "tensor", perm) for x, perm in zip(xs[1:], (NEXT, CORE, FAR))]


def spread(x, near):
    other = lax.ppermute(x, "tensor", CORE)
    far = lax.ppermute(near, "tensor", CORE)
    return x, near, other, far


def fold(mine, others):
    got = lax.ppermute(others, "tensor", CORE)
    rest = (mine[1].astype(F32) + got[1].astype(F32)).astype(BF16)
    return got, lax.ppermute(rest, "tensor", NEXT)


def expert_at(x, z, y):
    return (x * N_Z + z) * N_Y + y


def gather_dense(dense_up, dense_down, after):
    rows, units = dense_up.shape
    places = [(x, z, y) for x in range(N_X) for z in range(N_Z) for y in range(N_Y)]
    both = jnp.concatenate([dense_up, dense_down.T], axis=0)
    mate = lax.ppermute(both, "expert", [(expert_at(x, z, y), expert_at(1 - x, z, y)) for x, z, y in places])
    mate, _ = lax.optimization_barrier((mate, after))
    low = lax.axis_index("expert") < N_Z * N_Y
    pair = jnp.concatenate([jnp.where(low, both, mate), jnp.where(low, mate, both)])
    planes = [[expert_at(x, z, y) for z in range(N_Z) for y in range(N_Y)] for x in range(N_X)]
    out = lax.all_gather(pair, "expert", axis=0, tiled=True, axis_index_groups=planes)
    return out.reshape(N_Z, N_Y, N_X, 2, rows, units)


def local(tokens, expert_ids, gate_codes, dense_up, dense_down, expert_in, expert_out):
    rows_own, width = tokens.shape
    place = lax.axis_index("tensor")
    spot = place.reshape(1)
    n_tensor = lax.axis_size("tensor")
    group = rows_own * n_tensor
    n_experts = lax.axis_size("expert") * expert_in.shape[0]
    capacity = 5 * group // (2 * n_experts)
    part = width // n_tensor

    ids, codes = expert_ids.astype(jnp.int32).T, gate_codes.astype(jnp.int32).T
    meta = jnp.concatenate([ids, codes // 32, codes % 32, jnp.zeros((META - 6, rows_own), jnp.int32)])
    owner = jnp.arange(group, dtype=jnp.int32)[None, :] // rows_own
    meta = jnp.where(owner == place, jnp.tile(meta, (1, n_tensor)), 0).astype(BF16)
    meta = jnp.pad(meta, ((0, 0), (0, part - group)))
    grouped = swap(pack(spot, tokens, meta))
    routed, plan = dispatch(spot, grouped, n_experts, capacity)
    weights = gather_dense(dense_up, dense_down, plan)

    tokens_near = lax.ppermute(tokens, "tensor", NEXT)

    routed = lax.all_to_all(routed, "expert", split_axis=0, concat_axis=0, tiled=True)
    routed, tokens_near = lax.optimization_barrier((routed, tokens_near))
    start, terms, near, last = 0, [], None, None
    for size in SIZES:
        x = routed[start : start + size]
        start += size
        if near is not None:
            x, near = lax.optimization_barrier((x, near))
        near = lax.ppermute(x, "tensor", NEXT)
        own, beside, other, far = experts(spot, spread(x, near), expert_in[0], expert_out[0], capacity)
        if terms:
            near, own = lax.optimization_barrier((near, own))
        far = lax.ppermute(far, "tensor", CORE)
        other = lax.ppermute(other, "tensor", CORE)
        if terms:
            far, last = lax.optimization_barrier((far, last))
            terms[-1][-1] = last
        rest = (beside.astype(F32) + far.astype(F32)).astype(BF16)
        last = lax.ppermute(rest, "tensor", NEXT)
        terms.append([own, other, last])
    result = jnp.concatenate([(a.astype(F32) + b.astype(F32) + c.astype(F32)).astype(BF16) for a, b, c in terms])

    dense_own, result = lax.optimization_barrier((tokens, result))
    blocks = spread(tokens, tokens_near)
    mine, others = dense((dense_own,) + blocks[1:], weights)
    got, last = fold(mine, others)

    returned = lax.all_to_all(result, "expert", split_axis=0, concat_axis=0, tiled=True)
    pieces = swap(combine(spot, returned, plan, capacity))
    return finish(spot, tokens, mine, got, last, pieces)


def solution(mesh):
    return jax.shard_map(
        local,
        mesh=mesh,
        in_specs=(
            P(("expert", "tensor"), None),
            P(("expert", "tensor"), None),
            P(("expert", "tensor"), None),
            P("expert", "tensor"),
            P("tensor", "expert"),
            P("expert", None, "tensor"),
            P("expert", "tensor", None),
        ),
        out_specs=P(("expert", "tensor"), None),
        check_vma=False,
    )
```

```python
import functools

import jax
import jax.numpy as jnp
from jax import lax
from jax.experimental import pallas as pl
from jax.experimental.pallas import tpu as pltpu
from jax.sharding import PartitionSpec as P

F32 = jnp.float32
BF16 = jnp.bfloat16
CORE = [(0, 1), (1, 0), (2, 3), (3, 2)]
NEXT = [(0, 2), (2, 0), (1, 3), (3, 1)]
FAR = [(0, 3), (3, 0), (1, 2), (2, 1)]
N_X, N_Z, N_Y = 2, 8, 4
META = 16
MAIN = 8
LANES = 128
SIZES = (32, 32)
VMEM = 32 * 1024 * 1024


def dot(a, b, dims=((1,), (0,))):
    return lax.dot_general(a, b, (dims, ((), ())), preferred_element_type=F32)


def silu(v):
    return v / (1.0 + jnp.exp(-v))


def flip(step):
    return (0, 2, 1, 3)[step]


def at(place, step, size):
    return pl.multiple_of((place ^ flip(step)) * size, size)


def tiles_of(width, capacity):
    return width // LANES + capacity - MAIN


def put_tiles(ref, lead, scratch, main, tail, count, capacity):
    n, extra = main.shape[1] // LANES, capacity - MAIN
    for j in range(n):
        piece = main[:, j * LANES : (j + 1) * LANES].reshape(count, MAIN, LANES)
        ref[lead + (slice(None), j)] = piece.astype(BF16)
    for s in range(extra):
        for j in range(n):
            rows = pl.ds(s * MAIN + j, count, stride=extra * MAIN)
            scratch[rows, :] = tail[s * count : (s + 1) * count, j * LANES : (j + 1) * LANES]
    rest = scratch[...].reshape(count, extra, MAIN, LANES)
    for s in range(extra):
        ref[lead + (slice(None), n + s)] = rest[:, s].astype(BF16)


def take_tiles(ref, scratch, count, capacity):
    extra = capacity - MAIN
    n = ref.shape[1] - extra
    main = [ref[:, j].astype(F32).reshape(count * MAIN, LANES) for j in range(n)]
    scratch[...] = ref[:, n:].astype(F32).reshape(count * extra * MAIN, LANES)
    tail = []
    for s in range(extra):
        cut = [scratch[pl.ds(s * MAIN + j, count, stride=extra * MAIN), :] for j in range(n)]
        tail.append(jnp.concatenate(cut, axis=1))
    return jnp.concatenate([jnp.concatenate(main, axis=1)] + tail, axis=0).astype(BF16)


def clear(scratch):
    scratch[...] = jnp.zeros(scratch.shape, scratch.dtype)


SMEM = pl.BlockSpec(memory_space=pltpu.SMEM)
WHOLE = pl.BlockSpec(memory_space=pltpu.VMEM)
COST = pl.CostEstimate(flops=1, bytes_accessed=1, transcendentals=0)
LONG = pl.CostEstimate(flops=10_000_000_000_000, bytes_accessed=1, transcendentals=0)
PARAMS = pltpu.CompilerParams(vmem_limit_bytes=VMEM)


def pack_kernel(place_ref, tokens_ref, ids_ref, codes_ref, *out_refs):
    rows, part = tokens_ref.shape[0], out_refs[0].shape[1]
    group = len(out_refs) * rows
    codes = codes_ref[...]
    fields = [ids_ref[...], codes >> 5, codes & 31, jnp.zeros((META - 6, rows), jnp.int32)]
    fields = jnp.concatenate(fields, axis=0).astype(F32)
    lane = lax.broadcasted_iota(jnp.int32, (META, group), 1)
    own = (lane >= place_ref[0] * rows) & (lane < (place_ref[0] + 1) * rows)
    meta = jnp.where(own, jnp.concatenate([fields] * len(out_refs), axis=1), 0.0)
    meta = jnp.concatenate([meta, jnp.zeros((META, part - group), F32)], axis=1).astype(BF16)
    for step, out_ref in enumerate(out_refs):
        out_ref[:rows, :] = tokens_ref[:, pl.ds(at(place_ref[0], step, part), part)]
        out_ref[rows:, :] = meta


def pack(place, tokens, ids, codes):
    rows, width = tokens.shape
    block = jax.ShapeDtypeStruct((rows + META, width // 4), BF16)
    return pl.pallas_call(
        pack_kernel,
        in_specs=[SMEM] + [WHOLE] * 3,
        out_specs=[WHOLE] * 4,
        out_shape=[block] * 4,
        compiler_params=PARAMS,
        cost_estimate=COST,
        name="pack",
    )(place, tokens, ids, codes)


def pair_kernel(a_ref, b_ref, out_ref):
    rows = a_ref.shape[0]
    out_ref[:rows, :] = a_ref[...]
    out_ref[rows:, :] = b_ref[...]


def pair_up(a, b):
    return pl.pallas_call(
        pair_kernel,
        in_specs=[WHOLE] * 2,
        out_specs=WHOLE,
        out_shape=jax.ShapeDtypeStruct((2 * a.shape[0], a.shape[1]), a.dtype),
        compiler_params=PARAMS,
        cost_estimate=LONG,
        name="pair_up",
    )(a, b)


def dispatch_kernel(n_experts, capacity, place_ref, x0, x1, x2, x3, out_ref, plan_ref, tokens, scratch):
    rows = x0.shape[0] - META
    group = 4 * rows
    meta = jnp.zeros((META, group), F32)
    for step, x in enumerate((x0, x1, x2, x3)):
        meta = meta + x[rows:, :group].astype(F32)
        tokens[pl.ds(at(place_ref[0], step, rows), rows), :] = x[:rows, :]
    ids = [meta[k : k + 1].astype(jnp.int32) for k in range(2)]
    codes = [meta[2 + k : 3 + k] * 32.0 + meta[4 + k : 5 + k] for k in range(2)]
    names = lax.broadcasted_iota(jnp.int32, (n_experts, group), 0)
    hits = [(names == ids[k]).astype(F32) for k in range(2)]
    earlier = (
        lax.broadcasted_iota(jnp.int32, (group, group), 0)
        < lax.broadcasted_iota(jnp.int32, (group, group), 1)
    )
    before = dot((hits[0] + hits[1]).astype(BF16), earlier.astype(F32).astype(BF16))
    slots = [jnp.sum(hits[k] * before, axis=0, keepdims=True).astype(jnp.int32) for k in range(2)]
    in_main = [slots[k] < MAIN for k in range(2)]
    spot_main = [ids[k] * MAIN + slots[k] for k in range(2)]
    spot_tail = [(slots[k] - MAIN) * n_experts + ids[k] for k in range(2)]

    def placed(count, spots):
        row = lax.broadcasted_iota(jnp.int32, (count, group), 0)
        hit = jnp.where((row == spots[0]) | (row == spots[1]), 1.0, 0.0)
        return dot(hit.astype(BF16), tokens[...])

    main = placed(n_experts * MAIN, [jnp.where(in_main[k], spot_main[k], -1) for k in range(2)])
    tail = placed(
        n_experts * (capacity - MAIN), [jnp.where(in_main[k], -1, spot_tail[k]) for k in range(2)]
    )
    clear(scratch)
    put_tiles(out_ref, (), scratch, main, tail, n_experts, capacity)
    whole = codes[0] + codes[1]
    for k in range(2):
        row = jnp.where(in_main[k], spot_main[k], n_experts * MAIN + spot_tail[k])
        plan_ref[k : k + 1, :] = row.astype(F32)
        plan_ref[2 + k : 3 + k, :] = codes[k] / whole
    plan_ref[4:8, :] = jnp.zeros((4, group), F32)


def dispatch(place, xs, n_experts, capacity):
    rows_all, width = xs[0].shape
    group = 4 * (rows_all - META)
    return pl.pallas_call(
        functools.partial(dispatch_kernel, n_experts, capacity),
        in_specs=[SMEM] + [WHOLE] * 4,
        out_specs=[WHOLE] * 2,
        out_shape=[
            jax.ShapeDtypeStruct((n_experts, tiles_of(width, capacity), MAIN, LANES), BF16),
            jax.ShapeDtypeStruct((8, group), F32),
        ],
        scratch_shapes=[
            pltpu.VMEM((group, width), BF16),
            pltpu.VMEM((n_experts * (capacity - MAIN) * MAIN, LANES), F32),
        ],
        compiler_params=PARAMS,
        cost_estimate=COST,
        name="dispatch",
    )(place, *xs)


def experts_kernel(capacity, place_ref, x0, x1, x2, x3, up_ref, down_ref, o0, o1, o2, o3, x_all, scratch):
    count, tiles = x0.shape[:2]
    width = (tiles - capacity + MAIN) * LANES
    for step, x in enumerate((x0, x1, x2, x3)):
        x_all[:, pl.ds(at(place_ref[0], step, width), width)] = take_tiles(x, scratch, count, capacity)
    hidden = silu(dot(x_all[...], up_ref[...])).astype(BF16)
    clear(scratch)
    for step, ref in enumerate((o0, o1, o2, o3)):
        out = dot(hidden, down_ref[:, pl.ds(at(place_ref[0], step, width), width)])
        put_tiles(ref, (), scratch, out[: count * MAIN], out[count * MAIN :], count, capacity)


def experts(place, xs, up, down, capacity):
    count, tiles = xs[0].shape[:2]
    width, units = up.shape
    rows = count * capacity
    return pl.pallas_call(
        functools.partial(experts_kernel, capacity),
        in_specs=[SMEM] + [WHOLE] * 6,
        out_specs=[WHOLE] * 4,
        out_shape=[jax.ShapeDtypeStruct(xs[0].shape, BF16)] * 4,
        scratch_shapes=[
            pltpu.VMEM((rows, width), BF16),
            pltpu.VMEM((count * (capacity - MAIN) * MAIN, LANES), F32),
        ],
        compiler_params=PARAMS,
        cost_estimate=COST,
        name="experts",
    )(place, *xs, up, down)


def combine_kernel(capacity, place_ref, x_ref, plan_ref, o0, o1, o2, o3, scratch, routed):
    count = x_ref.shape[0]
    plan = plan_ref[...]
    group = plan.shape[1]
    values = take_tiles(x_ref, scratch, count, capacity)
    row = lax.broadcasted_iota(jnp.int32, (count * capacity, group), 0)
    gate = jnp.zeros((count * capacity, group), F32)
    for k in range(2):
        gate = gate + jnp.where(row == plan[k : k + 1].astype(jnp.int32), plan[2 + k : 3 + k], 0.0)
    high = gate.astype(BF16)
    low = (gate - high.astype(F32)).astype(BF16)
    routed[...] = (dot(high, values, ((0,), (0,))) + dot(low, values, ((0,), (0,)))).astype(BF16)
    for step, ref in enumerate((o0, o1, o2, o3)):
        ref[...] = routed[pl.ds(at(place_ref[0], step, group // 4), group // 4), :]


def combine(place, x, plan, capacity):
    count, tiles = x.shape[:2]
    width = (tiles - capacity + MAIN) * LANES
    group = plan.shape[1]
    return pl.pallas_call(
        functools.partial(combine_kernel, capacity),
        in_specs=[SMEM] + [WHOLE] * 2,
        out_specs=[WHOLE] * 4,
        out_shape=[jax.ShapeDtypeStruct((group // 4, width), BF16)] * 4,
        scratch_shapes=[
            pltpu.VMEM((count * (capacity - MAIN) * MAIN, LANES), F32),
            pltpu.VMEM((group, width), BF16),
        ],
        compiler_params=PARAMS,
        cost_estimate=COST,
        name="combine",
    )(place, x, plan)


def dense_kernel(x_mine, x_others, weights, mine_ref, others_ref, up_ref, down_ref, sems):
    z, half = weights.shape[0], weights.shape[0] // 2
    width = x_mine.shape[1]
    copies = [pltpu.make_async_copy(weights.at[:, :, i, 0], up_ref.at[i], sems.at[i]) for i in range(N_X)]
    for n in range(4):
        rows = pl.ds(n % 2 * half, half)
        copies.append(pltpu.make_async_copy(weights.at[rows, :, n // 2, 1], down_ref.at[n], sems.at[N_X + n]))
    for copy in copies:
        copy.start()

    def rows_of(block):
        return block.astype(F32).reshape(-1, block.shape[-1]).astype(BF16)

    pre = None
    for i in range(N_X):
        cut = slice(i * width // N_X, (i + 1) * width // N_X)
        x = jnp.concatenate([x_mine[:, cut], x_others[:, cut]], axis=0)
        copies[i].wait()
        part = dot(x, rows_of(up_ref[i]))
        pre = part if pre is None else pre + part
    hidden = silu(pre).astype(BF16)
    for n in range(4):
        cut = slice(n * width // 4, (n + 1) * width // 4)
        copies[N_X + n].wait()
        out = dot(hidden, rows_of(down_ref[n]), ((1,), (1,))).astype(BF16)
        out = out.reshape((4,) + mine_ref.shape[1:2] + (width // 4,))
        mine_ref[:, :, cut] = out[:2]
        others_ref[:, :, cut] = out[2:]


def dense(xs, weights):
    z, y, _, _, inner, units = weights.shape
    return pl.pallas_call(
        dense_kernel,
        in_specs=[WHOLE] * 2 + [pl.BlockSpec(memory_space=pltpu.HBM)],
        out_specs=[WHOLE] * 2,
        out_shape=[jax.ShapeDtypeStruct((2, xs[0].shape[0] // 2, xs[0].shape[1]), BF16)] * 2,
        scratch_shapes=[
            pltpu.VMEM((N_X, z, y, inner, units), BF16),
            pltpu.VMEM((4, z // 2, y, inner, units), BF16),
            pltpu.SemaphoreType.DMA((N_X + 4,)),
        ],
        compiler_params=PARAMS,
        cost_estimate=COST,
        name="dense",
    )(*xs, weights)


def finish_kernel(place_ref, tokens_ref, mine_ref, got_ref, last_ref, r0, r1, r2, r3, out_ref):
    part = r0.shape[1]
    for step, ref in enumerate((r0, r1, r2, r3)):
        columns = pl.ds(at(place_ref[0], step, part), part)
        total = tokens_ref[:, columns].astype(F32) + mine_ref[0, :, columns].astype(F32)
        total = total + got_ref[0, :, columns].astype(F32) + last_ref[:, columns].astype(F32)
        out_ref[:, columns] = (total + ref[...].astype(F32)).astype(BF16)


def finish(place, tokens, mine, got, last, routed):
    return pl.pallas_call(
        finish_kernel,
        in_specs=[SMEM] + [WHOLE] * 8,
        out_specs=WHOLE,
        out_shape=jax.ShapeDtypeStruct(tokens.shape, BF16),
        compiler_params=PARAMS,
        cost_estimate=COST,
        name="finish",
    )(place, tokens, mine, got, last, *routed)


def swap(xs):
    return [xs[0]] + [lax.ppermute(x, "tensor", perm) for x, perm in zip(xs[1:], (NEXT, CORE, FAR))]


def spread(x, near):
    other = lax.ppermute(x, "tensor", CORE)
    far = lax.ppermute(near, "tensor", CORE)
    return x, near, other, far


def fold(mine, others):
    got = lax.ppermute(others, "tensor", CORE)
    rest = (mine[1].astype(F32) + got[1].astype(F32)).astype(BF16)
    return got, lax.ppermute(rest, "tensor", NEXT)


def expert_at(x, z, y):
    return (x * N_Z + z) * N_Y + y


def gather_dense(dense_up, dense_down, after):
    rows, units = dense_up.shape
    places = [(x, z, y) for x in range(N_X) for z in range(N_Z) for y in range(N_Y)]
    both = jnp.concatenate([dense_up, dense_down.T], axis=0)
    mate = lax.ppermute(both, "expert", [(expert_at(x, z, y), expert_at(1 - x, z, y)) for x, z, y in places])
    mate, _ = lax.optimization_barrier((mate, after))
    low = lax.axis_index("expert") < N_Z * N_Y
    pair = jnp.concatenate([jnp.where(low, both, mate), jnp.where(low, mate, both)])
    planes = [[expert_at(x, z, y) for z in range(N_Z) for y in range(N_Y)] for x in range(N_X)]
    out = lax.all_gather(pair, "expert", axis=0, tiled=True, axis_index_groups=planes)
    return out.reshape(N_Z, N_Y, N_X, 2, rows, units)


def local(tokens, expert_ids, gate_codes, dense_up, dense_down, expert_in, expert_out):
    rows_own, width = tokens.shape
    place = lax.axis_index("tensor")
    spot = place.reshape(1)
    n_tensor = lax.axis_size("tensor")
    group = rows_own * n_tensor
    n_experts = lax.axis_size("expert") * expert_in.shape[0]
    capacity = 5 * group // (2 * n_experts)
    part = width // n_tensor

    grouped = swap(pack(spot, tokens, expert_ids.T, gate_codes.T))
    routed, plan = dispatch(spot, grouped, n_experts, capacity)
    weights = gather_dense(dense_up, dense_down, plan)

    tokens_pair = pair_up(tokens, lax.ppermute(tokens, "tensor", NEXT))

    routed = lax.all_to_all(routed, "expert", split_axis=0, concat_axis=0, tiled=True)
    tokens_by = tokens_pair, lax.ppermute(tokens_pair, "tensor", CORE)
    routed, tokens_by = lax.optimization_barrier((routed, tokens_by))
    start, terms, near, last = 0, [], None, None
    for size in SIZES:
        x = routed[start : start + size]
        start += size
        if near is not None:
            x, near = lax.optimization_barrier((x, near))
        near = lax.ppermute(x, "tensor", NEXT)
        own, beside, other, far = experts(spot, spread(x, near), expert_in[0], expert_out[0], capacity)
        if terms:
            near, own = lax.optimization_barrier((near, own))
        far = lax.ppermute(far, "tensor", CORE)
        other = lax.ppermute(other, "tensor", CORE)
        if terms:
            far, last = lax.optimization_barrier((far, last))
            terms[-1][-1] = last
        rest = (beside.astype(F32) + far.astype(F32)).astype(BF16)
        last = lax.ppermute(rest, "tensor", NEXT)
        terms.append([own, other, last])
    result = jnp.concatenate([(a.astype(F32) + b.astype(F32) + c.astype(F32)).astype(BF16) for a, b, c in terms])

    tokens_by, result = lax.optimization_barrier((tokens_by, result))
    mine, others = dense(tokens_by, weights)
    got, last = fold(mine, others)

    returned = lax.all_to_all(result, "expert", split_axis=0, concat_axis=0, tiled=True)
    pieces = swap(combine(spot, returned, plan, capacity))
    return finish(spot, tokens, mine, got, last, pieces)


def solution(mesh):
    return jax.shard_map(
        local,
        mesh=mesh,
        in_specs=(
            P(("expert", "tensor"), None),
            P(("expert", "tensor"), None),
            P(("expert", "tensor"), None),
            P("expert", "tensor"),
            P("tensor", "expert"),
            P("expert", None, "tensor"),
            P("expert", "tensor", None),
        ),
        out_specs=P(("expert", "tensor"), None),
        check_vma=False,
    )
```

```python
import functools

import jax
import jax.numpy as jnp
from jax import lax
from jax.experimental import pallas as pl
from jax.experimental.pallas import tpu as pltpu
from jax.sharding import PartitionSpec as P

F32 = jnp.float32
BF16 = jnp.bfloat16
CORE = [(0, 1), (1, 0), (2, 3), (3, 2)]
NEXT = [(0, 2), (2, 0), (1, 3), (3, 1)]
FAR = [(0, 3), (3, 0), (1, 2), (2, 1)]
N_X, N_Z, N_Y = 2, 8, 4
META = 16
MAIN = 8
LANES = 128
SIZES = (32, 32)
VMEM = 32 * 1024 * 1024


def dot(a, b, dims=((1,), (0,))):
    return lax.dot_general(a, b, (dims, ((), ())), preferred_element_type=F32)


def silu(v):
    return v / (1.0 + jnp.exp(-v))


def flip(step):
    return (0, 2, 1, 3)[step]


def at(place, step, size):
    return pl.multiple_of((place ^ flip(step)) * size, size)


def tiles_of(width, capacity):
    return width // LANES + capacity - MAIN


def put_tiles(ref, lead, scratch, main, tail, count, capacity):
    n, extra = main.shape[1] // LANES, capacity - MAIN
    for j in range(n):
        piece = main[:, j * LANES : (j + 1) * LANES].reshape(count, MAIN, LANES)
        ref[lead + (slice(None), j)] = piece.astype(BF16)
    for s in range(extra):
        for j in range(n):
            rows = pl.ds(s * MAIN + j, count, stride=extra * MAIN)
            scratch[rows, :] = tail[s * count : (s + 1) * count, j * LANES : (j + 1) * LANES]
    rest = scratch[...].reshape(count, extra, MAIN, LANES)
    for s in range(extra):
        ref[lead + (slice(None), n + s)] = rest[:, s].astype(BF16)


def take_tiles(ref, scratch, count, capacity):
    extra = capacity - MAIN
    n = ref.shape[1] - extra
    main = [ref[:, j].astype(F32).reshape(count * MAIN, LANES) for j in range(n)]
    scratch[...] = ref[:, n:].astype(F32).reshape(count * extra * MAIN, LANES)
    tail = []
    for s in range(extra):
        cut = [scratch[pl.ds(s * MAIN + j, count, stride=extra * MAIN), :] for j in range(n)]
        tail.append(jnp.concatenate(cut, axis=1))
    return jnp.concatenate([jnp.concatenate(main, axis=1)] + tail, axis=0).astype(BF16)


def clear(scratch):
    scratch[...] = jnp.zeros(scratch.shape, scratch.dtype)


SMEM = pl.BlockSpec(memory_space=pltpu.SMEM)
WHOLE = pl.BlockSpec(memory_space=pltpu.VMEM)
COST = pl.CostEstimate(flops=1, bytes_accessed=1, transcendentals=0)
LONG = pl.CostEstimate(flops=10_000_000_000_000, bytes_accessed=1, transcendentals=0)
PARAMS = pltpu.CompilerParams(vmem_limit_bytes=VMEM)


def pack_kernel(place_ref, tokens_ref, pairs_ref, *out_refs):
    rows, part = tokens_ref.shape[0], out_refs[0].shape[1]
    group = len(out_refs) * rows
    ids, codes = pairs_ref[:2, :], pairs_ref[2:4, :]
    fields = [ids, codes >> 5, codes & 31, jnp.zeros((META - 6, rows), jnp.int32)]
    fields = jnp.concatenate(fields, axis=0).astype(F32)
    lane = lax.broadcasted_iota(jnp.int32, (META, group), 1)
    own = (lane >= place_ref[0] * rows) & (lane < (place_ref[0] + 1) * rows)
    meta = jnp.where(own, jnp.concatenate([fields] * len(out_refs), axis=1), 0.0)
    meta = jnp.concatenate([meta, jnp.zeros((META, part - group), F32)], axis=1).astype(BF16)
    for step, out_ref in enumerate(out_refs):
        out_ref[:rows, :] = tokens_ref[:, pl.ds(at(place_ref[0], step, part), part)]
        out_ref[rows:, :] = meta


def pack(place, tokens, pairs):
    rows, width = tokens.shape
    block = jax.ShapeDtypeStruct((rows + META, width // 4), BF16)
    return pl.pallas_call(
        pack_kernel,
        in_specs=[SMEM] + [WHOLE] * 2,
        out_specs=[WHOLE] * 4,
        out_shape=[block] * 4,
        compiler_params=PARAMS,
        cost_estimate=COST,
        name="pack",
    )(place, tokens, pairs)


def pair_kernel(a_ref, b_ref, out_ref):
    rows = a_ref.shape[0]
    out_ref[:rows, :] = a_ref[...]
    out_ref[rows:, :] = b_ref[...]


def pair_up(a, b):
    return pl.pallas_call(
        pair_kernel,
        in_specs=[WHOLE] * 2,
        out_specs=WHOLE,
        out_shape=jax.ShapeDtypeStruct((2 * a.shape[0], a.shape[1]), a.dtype),
        compiler_params=PARAMS,
        cost_estimate=LONG,
        name="pair_up",
    )(a, b)


def dispatch_kernel(n_experts, capacity, place_ref, x0, x1, x2, x3, out_ref, plan_ref, tokens, scratch):
    rows = x0.shape[0] - META
    group = 4 * rows
    meta = jnp.zeros((META, group), F32)
    for step, x in enumerate((x0, x1, x2, x3)):
        meta = meta + x[rows:, :group].astype(F32)
        tokens[pl.ds(at(place_ref[0], step, rows), rows), :] = x[:rows, :]
    ids = [meta[k : k + 1].astype(jnp.int32) for k in range(2)]
    codes = [meta[2 + k : 3 + k] * 32.0 + meta[4 + k : 5 + k] for k in range(2)]
    names = lax.broadcasted_iota(jnp.int32, (n_experts, group), 0)
    hits = [(names == ids[k]).astype(F32) for k in range(2)]
    earlier = (
        lax.broadcasted_iota(jnp.int32, (group, group), 0)
        < lax.broadcasted_iota(jnp.int32, (group, group), 1)
    )
    before = dot((hits[0] + hits[1]).astype(BF16), earlier.astype(F32).astype(BF16))
    slots = [jnp.sum(hits[k] * before, axis=0, keepdims=True).astype(jnp.int32) for k in range(2)]
    in_main = [slots[k] < MAIN for k in range(2)]
    spot_main = [ids[k] * MAIN + slots[k] for k in range(2)]
    spot_tail = [(slots[k] - MAIN) * n_experts + ids[k] for k in range(2)]

    def placed(count, spots):
        row = lax.broadcasted_iota(jnp.int32, (count, group), 0)
        hit = jnp.where((row == spots[0]) | (row == spots[1]), 1.0, 0.0)
        return dot(hit.astype(BF16), tokens[...])

    main = placed(n_experts * MAIN, [jnp.where(in_main[k], spot_main[k], -1) for k in range(2)])
    tail = placed(
        n_experts * (capacity - MAIN), [jnp.where(in_main[k], -1, spot_tail[k]) for k in range(2)]
    )
    clear(scratch)
    put_tiles(out_ref, (), scratch, main, tail, n_experts, capacity)
    whole = codes[0] + codes[1]
    for k in range(2):
        row = jnp.where(in_main[k], spot_main[k], n_experts * MAIN + spot_tail[k])
        plan_ref[k : k + 1, :] = row.astype(F32)
        plan_ref[2 + k : 3 + k, :] = codes[k] / whole
    plan_ref[4:8, :] = jnp.zeros((4, group), F32)


def dispatch(place, xs, n_experts, capacity):
    rows_all, width = xs[0].shape
    group = 4 * (rows_all - META)
    return pl.pallas_call(
        functools.partial(dispatch_kernel, n_experts, capacity),
        in_specs=[SMEM] + [WHOLE] * 4,
        out_specs=[WHOLE] * 2,
        out_shape=[
            jax.ShapeDtypeStruct((n_experts, tiles_of(width, capacity), MAIN, LANES), BF16),
            jax.ShapeDtypeStruct((8, group), F32),
        ],
        scratch_shapes=[
            pltpu.VMEM((group, width), BF16),
            pltpu.VMEM((n_experts * (capacity - MAIN) * MAIN, LANES), F32),
        ],
        compiler_params=PARAMS,
        cost_estimate=COST,
        name="dispatch",
    )(place, *xs)


def experts_kernel(capacity, place_ref, x0, x1, x2, x3, up_ref, down_ref, o0, o1, o2, o3, x_all, scratch):
    count, tiles = x0.shape[:2]
    width = (tiles - capacity + MAIN) * LANES
    for step, x in enumerate((x0, x1, x2, x3)):
        x_all[:, pl.ds(at(place_ref[0], step, width), width)] = take_tiles(x, scratch, count, capacity)
    hidden = silu(dot(x_all[...], up_ref[...])).astype(BF16)
    clear(scratch)
    for step, ref in enumerate((o0, o1, o2, o3)):
        out = dot(hidden, down_ref[:, pl.ds(at(place_ref[0], step, width), width)])
        put_tiles(ref, (), scratch, out[: count * MAIN], out[count * MAIN :], count, capacity)


def experts(place, xs, up, down, capacity):
    count, tiles = xs[0].shape[:2]
    width, units = up.shape
    rows = count * capacity
    return pl.pallas_call(
        functools.partial(experts_kernel, capacity),
        in_specs=[SMEM] + [WHOLE] * 6,
        out_specs=[WHOLE] * 4,
        out_shape=[jax.ShapeDtypeStruct(xs[0].shape, BF16)] * 4,
        scratch_shapes=[
            pltpu.VMEM((rows, width), BF16),
            pltpu.VMEM((count * (capacity - MAIN) * MAIN, LANES), F32),
        ],
        compiler_params=PARAMS,
        cost_estimate=COST,
        name="experts",
    )(place, *xs, up, down)


def total_kernel(first_ref, a_ref, b_ref, c_ref, out_ref):
    done = first_ref.shape[0]
    out_ref[:done] = first_ref[...]
    total = a_ref[...].astype(F32) + b_ref[...].astype(F32) + c_ref[...].astype(F32)
    out_ref[done:] = total.astype(BF16)


def total_of(first, terms):
    return pl.pallas_call(
        total_kernel,
        in_specs=[WHOLE] * 4,
        out_specs=WHOLE,
        out_shape=jax.ShapeDtypeStruct((first.shape[0] + terms[0].shape[0],) + first.shape[1:], BF16),
        compiler_params=PARAMS,
        cost_estimate=COST,
        name="total",
    )(first, *terms)


def combine_kernel(capacity, place_ref, x_ref, plan_ref, o0, o1, o2, o3, scratch, routed):
    count = x_ref.shape[0]
    plan = plan_ref[...]
    group = plan.shape[1]
    values = take_tiles(x_ref, scratch, count, capacity)
    row = lax.broadcasted_iota(jnp.int32, (count * capacity, group), 0)
    gate = jnp.zeros((count * capacity, group), F32)
    for k in range(2):
        gate = gate + jnp.where(row == plan[k : k + 1].astype(jnp.int32), plan[2 + k : 3 + k], 0.0)
    high = gate.astype(BF16)
    low = (gate - high.astype(F32)).astype(BF16)
    routed[...] = (dot(high, values, ((0,), (0,))) + dot(low, values, ((0,), (0,)))).astype(BF16)
    for step, ref in enumerate((o0, o1, o2, o3)):
        ref[...] = routed[pl.ds(at(place_ref[0], step, group // 4), group // 4), :]


def combine(place, x, plan, capacity):
    count, tiles = x.shape[:2]
    width = (tiles - capacity + MAIN) * LANES
    group = plan.shape[1]
    return pl.pallas_call(
        functools.partial(combine_kernel, capacity),
        in_specs=[SMEM] + [WHOLE] * 2,
        out_specs=[WHOLE] * 4,
        out_shape=[jax.ShapeDtypeStruct((group // 4, width), BF16)] * 4,
        scratch_shapes=[
            pltpu.VMEM((count * (capacity - MAIN) * MAIN, LANES), F32),
            pltpu.VMEM((group, width), BF16),
        ],
        compiler_params=PARAMS,
        cost_estimate=COST,
        name="combine",
    )(place, x, plan)


def dense_kernel(x_mine, x_others, weights, mine_ref, others_ref, up_ref, down_ref, sems):
    z, half = weights.shape[0], weights.shape[0] // 2
    width = x_mine.shape[1]
    copies = [pltpu.make_async_copy(weights.at[:, :, i, 0], up_ref.at[i], sems.at[i]) for i in range(N_X)]
    for n in range(4):
        rows = pl.ds(n % 2 * half, half)
        copies.append(pltpu.make_async_copy(weights.at[rows, :, n // 2, 1], down_ref.at[n], sems.at[N_X + n]))
    for copy in copies:
        copy.start()

    def rows_of(block):
        return block.astype(F32).reshape(-1, block.shape[-1]).astype(BF16)

    pre = None
    for i in range(N_X):
        cut = slice(i * width // N_X, (i + 1) * width // N_X)
        x = jnp.concatenate([x_mine[:, cut], x_others[:, cut]], axis=0)
        copies[i].wait()
        part = dot(x, rows_of(up_ref[i]))
        pre = part if pre is None else pre + part
    hidden = silu(pre).astype(BF16)
    for n in range(4):
        cut = slice(n * width // 4, (n + 1) * width // 4)
        copies[N_X + n].wait()
        out = dot(hidden, rows_of(down_ref[n]), ((1,), (1,))).astype(BF16)
        out = out.reshape((4,) + mine_ref.shape[1:2] + (width // 4,))
        mine_ref[:, :, cut] = out[:2]
        others_ref[:, :, cut] = out[2:]


def dense(xs, weights):
    z, y, _, _, inner, units = weights.shape
    return pl.pallas_call(
        dense_kernel,
        in_specs=[WHOLE] * 2 + [pl.BlockSpec(memory_space=pltpu.HBM)],
        out_specs=[WHOLE] * 2,
        out_shape=[jax.ShapeDtypeStruct((2, xs[0].shape[0] // 2, xs[0].shape[1]), BF16)] * 2,
        scratch_shapes=[
            pltpu.VMEM((N_X, z, y, inner, units), BF16),
            pltpu.VMEM((4, z // 2, y, inner, units), BF16),
            pltpu.SemaphoreType.DMA((N_X + 4,)),
        ],
        compiler_params=PARAMS,
        cost_estimate=COST,
        name="dense",
    )(*xs, weights)


def finish_kernel(place_ref, tokens_ref, mine_ref, got_ref, last_ref, r0, r1, r2, r3, out_ref):
    part = r0.shape[1]
    for step, ref in enumerate((r0, r1, r2, r3)):
        columns = pl.ds(at(place_ref[0], step, part), part)
        total = tokens_ref[:, columns].astype(F32) + mine_ref[0, :, columns].astype(F32)
        total = total + got_ref[0, :, columns].astype(F32) + last_ref[:, columns].astype(F32)
        out_ref[:, columns] = (total + ref[...].astype(F32)).astype(BF16)


def finish(place, tokens, mine, got, last, routed):
    return pl.pallas_call(
        finish_kernel,
        in_specs=[SMEM] + [WHOLE] * 8,
        out_specs=WHOLE,
        out_shape=jax.ShapeDtypeStruct(tokens.shape, BF16),
        compiler_params=PARAMS,
        cost_estimate=COST,
        name="finish",
    )(place, tokens, mine, got, last, *routed)


def swap(xs):
    return [xs[0]] + [lax.ppermute(x, "tensor", perm) for x, perm in zip(xs[1:], (NEXT, CORE, FAR))]


def spread(x, near):
    other = lax.ppermute(x, "tensor", CORE)
    far = lax.ppermute(near, "tensor", CORE)
    return x, near, other, far


def fold(mine, others):
    got = lax.ppermute(others, "tensor", CORE)
    rest = (mine[1].astype(F32) + got[1].astype(F32)).astype(BF16)
    return got, lax.ppermute(rest, "tensor", NEXT)


def expert_at(x, z, y):
    return (x * N_Z + z) * N_Y + y


def gather_dense(dense_up, dense_down, before, after):
    rows, units = dense_up.shape
    places = [(x, z, y) for x in range(N_X) for z in range(N_Z) for y in range(N_Y)]
    both = jnp.concatenate([dense_up, dense_down.T], axis=0)
    both, _ = lax.optimization_barrier((both, before))
    mate = lax.ppermute(both, "expert", [(expert_at(x, z, y), expert_at(1 - x, z, y)) for x, z, y in places])
    mate, _ = lax.optimization_barrier((mate, after))
    low = lax.axis_index("expert") < N_Z * N_Y
    pair = jnp.concatenate([jnp.where(low, both, mate), jnp.where(low, mate, both)])
    planes = [[expert_at(x, z, y) for z in range(N_Z) for y in range(N_Y)] for x in range(N_X)]
    out = lax.all_gather(pair, "expert", axis=0, tiled=True, axis_index_groups=planes)
    return out.reshape(N_Z, N_Y, N_X, 2, rows, units)


def local(tokens, expert_ids, gate_codes, dense_up, dense_down, expert_in, expert_out):
    rows_own, width = tokens.shape
    place = lax.axis_index("tensor")
    spot = place.reshape(1)
    n_tensor = lax.axis_size("tensor")
    group = rows_own * n_tensor
    n_experts = lax.axis_size("expert") * expert_in.shape[0]
    capacity = 5 * group // (2 * n_experts)
    part = width // n_tensor

    grouped = swap(pack(spot, tokens, jnp.concatenate([expert_ids.T, gate_codes.T], axis=0)))
    routed, plan = dispatch(spot, grouped, n_experts, capacity)
    weights = gather_dense(dense_up, dense_down, grouped, plan)

    later, _ = lax.optimization_barrier((tokens, grouped))
    tokens_pair = pair_up(tokens, lax.ppermute(later, "tensor", NEXT))

    routed = lax.all_to_all(routed, "expert", split_axis=0, concat_axis=0, tiled=True)
    tokens_by = tokens_pair, lax.ppermute(tokens_pair, "tensor", CORE)
    routed, tokens_by = lax.optimization_barrier((routed, tokens_by))
    start, terms, near, last = 0, [], None, None
    for size in SIZES:
        x = routed[start : start + size]
        start += size
        if near is not None:
            x, near = lax.optimization_barrier((x, near))
        near = lax.ppermute(x, "tensor", NEXT)
        own, beside, other, far = experts(spot, spread(x, near), expert_in[0], expert_out[0], capacity)
        if terms:
            near, own = lax.optimization_barrier((near, own))
        far = lax.ppermute(far, "tensor", CORE)
        other = lax.ppermute(other, "tensor", CORE)
        if terms:
            far, last = lax.optimization_barrier((far, last))
            terms[-1][-1] = last
        rest = (beside.astype(F32) + far.astype(F32)).astype(BF16)
        last = lax.ppermute(rest, "tensor", NEXT)
        terms.append([own, other, last])
    a, b, c = terms[0]
    result = total_of((a.astype(F32) + b.astype(F32) + c.astype(F32)).astype(BF16), terms[1])

    tokens_by, result = lax.optimization_barrier((tokens_by, result))
    mine, others = dense(tokens_by, weights)
    got, last = fold(mine, others)

    returned = lax.all_to_all(result, "expert", split_axis=0, concat_axis=0, tiled=True)
    pieces = swap(combine(spot, returned, plan, capacity))
    return finish(spot, tokens, mine, got, last, pieces)


def solution(mesh):
    return jax.shard_map(
        local,
        mesh=mesh,
        in_specs=(
            P(("expert", "tensor"), None),
            P(("expert", "tensor"), None),
            P(("expert", "tensor"), None),
            P("expert", "tensor"),
            P("tensor", "expert"),
            P("expert", None, "tensor"),
            P("expert", "tensor", None),
        ),
        out_specs=P(("expert", "tensor"), None),
        check_vma=False,
    )
```

```python
import functools

import jax
import jax.numpy as jnp
from jax import lax
from jax.experimental import pallas as pl
from jax.experimental.pallas import tpu as pltpu
from jax.sharding import PartitionSpec as P

F32 = jnp.float32
BF16 = jnp.bfloat16
CORE = [(0, 1), (1, 0), (2, 3), (3, 2)]
NEXT = [(0, 2), (2, 0), (1, 3), (3, 1)]
FAR = [(0, 3), (3, 0), (1, 2), (2, 1)]
N_X, N_Z, N_Y = 2, 8, 4
META = 16
MAIN = 8
LANES = 128
SIZES = (32, 32)
VMEM = 16 * 1024 * 1024


def dot(a, b, dims=((1,), (0,))):
    return lax.dot_general(a, b, (dims, ((), ())), preferred_element_type=F32)


def silu(v):
    return v / (1.0 + jnp.exp(-v))


def flip(step):
    return (0, 2, 1, 3)[step]


def at(place, step, size):
    return pl.multiple_of((place ^ flip(step)) * size, size)


def tiles_of(width, capacity):
    return width // LANES + capacity - MAIN


def put_tiles(ref, lead, scratch, main, tail, count, capacity):
    n, extra = main.shape[1] // LANES, capacity - MAIN
    for j in range(n):
        piece = main[:, j * LANES : (j + 1) * LANES].reshape(count, MAIN, LANES)
        ref[lead + (slice(None), j)] = piece.astype(BF16)
    for s in range(extra):
        for j in range(n):
            rows = pl.ds(s * MAIN + j, count, stride=extra * MAIN)
            scratch[rows, :] = tail[s * count : (s + 1) * count, j * LANES : (j + 1) * LANES]
    rest = scratch[...].reshape(count, extra, MAIN, LANES)
    for s in range(extra):
        ref[lead + (slice(None), n + s)] = rest[:, s].astype(BF16)


def take_tiles(ref, scratch, count, capacity):
    extra = capacity - MAIN
    n = ref.shape[1] - extra
    main = [ref[:, j].astype(F32).reshape(count * MAIN, LANES) for j in range(n)]
    scratch[...] = ref[:, n:].astype(F32).reshape(count * extra * MAIN, LANES)
    tail = []
    for s in range(extra):
        cut = [scratch[pl.ds(s * MAIN + j, count, stride=extra * MAIN), :] for j in range(n)]
        tail.append(jnp.concatenate(cut, axis=1))
    return jnp.concatenate([jnp.concatenate(main, axis=1)] + tail, axis=0).astype(BF16)


def clear(scratch):
    scratch[...] = jnp.zeros(scratch.shape, scratch.dtype)


SMEM = pl.BlockSpec(memory_space=pltpu.SMEM)
WHOLE = pl.BlockSpec(memory_space=pltpu.VMEM)
COST = pl.CostEstimate(flops=1, bytes_accessed=1, transcendentals=0)
LONG = pl.CostEstimate(flops=10_000_000_000_000, bytes_accessed=1, transcendentals=0)
PARAMS = pltpu.CompilerParams(vmem_limit_bytes=VMEM)


def pack_kernel(place_ref, tokens_ref, pairs_ref, *out_refs):
    rows, part = tokens_ref.shape[0], out_refs[0].shape[1]
    group = len(out_refs) * rows
    ids, codes = pairs_ref[:2, :], pairs_ref[2:4, :]
    fields = [ids, codes >> 5, codes & 31, jnp.zeros((META - 6, rows), jnp.int32)]
    fields = jnp.concatenate(fields, axis=0).astype(F32)
    lane = lax.broadcasted_iota(jnp.int32, (META, group), 1)
    own = (lane >= place_ref[0] * rows) & (lane < (place_ref[0] + 1) * rows)
    meta = jnp.where(own, jnp.concatenate([fields] * len(out_refs), axis=1), 0.0)
    meta = jnp.concatenate([meta, jnp.zeros((META, part - group), F32)], axis=1).astype(BF16)
    for step, out_ref in enumerate(out_refs):
        out_ref[:rows, :] = tokens_ref[:, pl.ds(at(place_ref[0], step, part), part)]
        out_ref[rows:, :] = meta


def pack(place, tokens, pairs):
    rows, width = tokens.shape
    block = jax.ShapeDtypeStruct((rows + META, width // 4), BF16)
    return pl.pallas_call(
        pack_kernel,
        in_specs=[SMEM] + [WHOLE] * 2,
        out_specs=[WHOLE] * 4,
        out_shape=[block] * 4,
        compiler_params=PARAMS,
        cost_estimate=COST,
        name="pack",
    )(place, tokens, pairs)


def pair_kernel(a_ref, b_ref, out_ref):
    rows = a_ref.shape[0]
    out_ref[:rows, :] = a_ref[...]
    out_ref[rows:, :] = b_ref[...]


def pair_up(a, b):
    return pl.pallas_call(
        pair_kernel,
        in_specs=[WHOLE] * 2,
        out_specs=WHOLE,
        out_shape=jax.ShapeDtypeStruct((2 * a.shape[0], a.shape[1]), a.dtype),
        compiler_params=PARAMS,
        cost_estimate=LONG,
        name="pair_up",
    )(a, b)


def dispatch_kernel(n_experts, capacity, place_ref, x0, x1, x2, x3, out_ref, plan_ref, tokens, scratch):
    rows = x0.shape[0] - META
    group = 4 * rows
    meta = jnp.zeros((META, group), F32)
    for step, x in enumerate((x0, x1, x2, x3)):
        meta = meta + x[rows:, :group].astype(F32)
        tokens[pl.ds(at(place_ref[0], step, rows), rows), :] = x[:rows, :]
    ids = [meta[k : k + 1].astype(jnp.int32) for k in range(2)]
    codes = [meta[2 + k : 3 + k] * 32.0 + meta[4 + k : 5 + k] for k in range(2)]
    names = lax.broadcasted_iota(jnp.int32, (n_experts, group), 0)
    hits = [(names == ids[k]).astype(F32) for k in range(2)]
    earlier = (
        lax.broadcasted_iota(jnp.int32, (group, group), 0)
        < lax.broadcasted_iota(jnp.int32, (group, group), 1)
    )
    before = dot((hits[0] + hits[1]).astype(BF16), earlier.astype(F32).astype(BF16))
    slots = [jnp.sum(hits[k] * before, axis=0, keepdims=True).astype(jnp.int32) for k in range(2)]
    in_main = [slots[k] < MAIN for k in range(2)]
    spot_main = [ids[k] * MAIN + slots[k] for k in range(2)]
    spot_tail = [(slots[k] - MAIN) * n_experts + ids[k] for k in range(2)]

    def placed(count, spots):
        row = lax.broadcasted_iota(jnp.int32, (count, group), 0)
        hit = jnp.where((row == spots[0]) | (row == spots[1]), 1.0, 0.0)
        return dot(hit.astype(BF16), tokens[...])

    main = placed(n_experts * MAIN, [jnp.where(in_main[k], spot_main[k], -1) for k in range(2)])
    tail = placed(
        n_experts * (capacity - MAIN), [jnp.where(in_main[k], -1, spot_tail[k]) for k in range(2)]
    )
    clear(scratch)
    put_tiles(out_ref, (), scratch, main, tail, n_experts, capacity)
    whole = codes[0] + codes[1]
    for k in range(2):
        row = jnp.where(in_main[k], spot_main[k], n_experts * MAIN + spot_tail[k])
        plan_ref[k : k + 1, :] = row.astype(F32)
        plan_ref[2 + k : 3 + k, :] = codes[k] / whole
    plan_ref[4:8, :] = jnp.zeros((4, group), F32)


def dispatch(place, xs, n_experts, capacity):
    rows_all, width = xs[0].shape
    group = 4 * (rows_all - META)
    return pl.pallas_call(
        functools.partial(dispatch_kernel, n_experts, capacity),
        in_specs=[SMEM] + [WHOLE] * 4,
        out_specs=[WHOLE] * 2,
        out_shape=[
            jax.ShapeDtypeStruct((n_experts, tiles_of(width, capacity), MAIN, LANES), BF16),
            jax.ShapeDtypeStruct((8, group), F32),
        ],
        scratch_shapes=[
            pltpu.VMEM((group, width), BF16),
            pltpu.VMEM((n_experts * (capacity - MAIN) * MAIN, LANES), F32),
        ],
        compiler_params=PARAMS,
        cost_estimate=COST,
        name="dispatch",
    )(place, *xs)


def experts_kernel(capacity, place_ref, x0, x1, x2, x3, up_ref, down_ref, o0, o1, o2, o3, x_all, scratch):
    count, tiles = x0.shape[:2]
    width = (tiles - capacity + MAIN) * LANES
    for step, x in enumerate((x0, x1, x2, x3)):
        x_all[:, pl.ds(at(place_ref[0], step, width), width)] = take_tiles(x, scratch, count, capacity)
    hidden = silu(dot(x_all[...], up_ref[...])).astype(BF16)
    clear(scratch)
    for step, ref in enumerate((o0, o1, o2, o3)):
        out = dot(hidden, down_ref[:, pl.ds(at(place_ref[0], step, width), width)])
        put_tiles(ref, (), scratch, out[: count * MAIN], out[count * MAIN :], count, capacity)


def experts(place, xs, up, down, capacity):
    count, tiles = xs[0].shape[:2]
    width, units = up.shape
    rows = count * capacity
    return pl.pallas_call(
        functools.partial(experts_kernel, capacity),
        in_specs=[SMEM] + [WHOLE] * 6,
        out_specs=[WHOLE] * 4,
        out_shape=[jax.ShapeDtypeStruct(xs[0].shape, BF16)] * 4,
        scratch_shapes=[
            pltpu.VMEM((rows, width), BF16),
            pltpu.VMEM((count * (capacity - MAIN) * MAIN, LANES), F32),
        ],
        compiler_params=PARAMS,
        cost_estimate=COST,
        name="experts",
    )(place, *xs, up, down)


def total_kernel(first_ref, a_ref, b_ref, c_ref, out_ref):
    done = first_ref.shape[0]
    out_ref[:done] = first_ref[...]
    total = a_ref[...].astype(F32) + b_ref[...].astype(F32) + c_ref[...].astype(F32)
    out_ref[done:] = total.astype(BF16)


def total_of(first, terms):
    return pl.pallas_call(
        total_kernel,
        in_specs=[WHOLE] * 4,
        out_specs=WHOLE,
        out_shape=jax.ShapeDtypeStruct((first.shape[0] + terms[0].shape[0],) + first.shape[1:], BF16),
        compiler_params=PARAMS,
        cost_estimate=COST,
        name="total",
    )(first, *terms)


def combine_kernel(capacity, place_ref, x_ref, plan_ref, o0, o1, o2, o3, scratch, routed):
    count = x_ref.shape[0]
    plan = plan_ref[...]
    group = plan.shape[1]
    values = take_tiles(x_ref, scratch, count, capacity)
    row = lax.broadcasted_iota(jnp.int32, (count * capacity, group), 0)
    gate = jnp.zeros((count * capacity, group), F32)
    for k in range(2):
        gate = gate + jnp.where(row == plan[k : k + 1].astype(jnp.int32), plan[2 + k : 3 + k], 0.0)
    high = gate.astype(BF16)
    low = (gate - high.astype(F32)).astype(BF16)
    routed[...] = (dot(high, values, ((0,), (0,))) + dot(low, values, ((0,), (0,)))).astype(BF16)
    for step, ref in enumerate((o0, o1, o2, o3)):
        ref[...] = routed[pl.ds(at(place_ref[0], step, group // 4), group // 4), :]


def combine(place, x, plan, capacity):
    count, tiles = x.shape[:2]
    width = (tiles - capacity + MAIN) * LANES
    group = plan.shape[1]
    return pl.pallas_call(
        functools.partial(combine_kernel, capacity),
        in_specs=[SMEM] + [WHOLE] * 2,
        out_specs=[WHOLE] * 4,
        out_shape=[jax.ShapeDtypeStruct((group // 4, width), BF16)] * 4,
        scratch_shapes=[
            pltpu.VMEM((count * (capacity - MAIN) * MAIN, LANES), F32),
            pltpu.VMEM((group, width), BF16),
        ],
        compiler_params=PARAMS,
        cost_estimate=COST,
        name="combine",
    )(place, x, plan)


def dense_kernel(x_mine, x_others, weights, mine_ref, others_ref, up_ref, down_ref, sems):
    z, half = weights.shape[0], weights.shape[0] // 2
    width = x_mine.shape[1]
    copies = [pltpu.make_async_copy(weights.at[:, :, i, 0], up_ref.at[i], sems.at[i]) for i in range(N_X)]
    for n in range(4):
        rows = pl.ds(n % 2 * half, half)
        copies.append(pltpu.make_async_copy(weights.at[rows, :, n // 2, 1], down_ref.at[n], sems.at[N_X + n]))
    for copy in copies:
        copy.start()

    def rows_of(block):
        return block.astype(F32).reshape(-1, block.shape[-1]).astype(BF16)

    pre = None
    for i in range(N_X):
        cut = slice(i * width // N_X, (i + 1) * width // N_X)
        x = jnp.concatenate([x_mine[:, cut], x_others[:, cut]], axis=0)
        copies[i].wait()
        part = dot(x, rows_of(up_ref[i]))
        pre = part if pre is None else pre + part
    hidden = silu(pre).astype(BF16)
    for n in range(4):
        cut = slice(n * width // 4, (n + 1) * width // 4)
        copies[N_X + n].wait()
        out = dot(hidden, rows_of(down_ref[n]), ((1,), (1,))).astype(BF16)
        out = out.reshape((4,) + mine_ref.shape[1:2] + (width // 4,))
        mine_ref[:, :, cut] = out[:2]
        others_ref[:, :, cut] = out[2:]


def dense(xs, weights):
    z, y, _, _, inner, units = weights.shape
    return pl.pallas_call(
        dense_kernel,
        in_specs=[WHOLE] * 2 + [pl.BlockSpec(memory_space=pltpu.HBM)],
        out_specs=[WHOLE] * 2,
        out_shape=[jax.ShapeDtypeStruct((2, xs[0].shape[0] // 2, xs[0].shape[1]), BF16)] * 2,
        scratch_shapes=[
            pltpu.VMEM((N_X, z, y, inner, units), BF16),
            pltpu.VMEM((4, z // 2, y, inner, units), BF16),
            pltpu.SemaphoreType.DMA((N_X + 4,)),
        ],
        compiler_params=pltpu.CompilerParams(vmem_limit_bytes=56 * 1024 * 1024),
        cost_estimate=COST,
        name="dense",
    )(*xs, weights)


def finish_kernel(place_ref, tokens_ref, mine_ref, got_ref, last_ref, r0, r1, r2, r3, out_ref):
    part = r0.shape[1]
    for step, ref in enumerate((r0, r1, r2, r3)):
        columns = pl.ds(at(place_ref[0], step, part), part)
        total = tokens_ref[:, columns].astype(F32) + mine_ref[0, :, columns].astype(F32)
        total = total + got_ref[0, :, columns].astype(F32) + last_ref[:, columns].astype(F32)
        out_ref[:, columns] = (total + ref[...].astype(F32)).astype(BF16)


def finish(place, tokens, mine, got, last, routed):
    return pl.pallas_call(
        finish_kernel,
        in_specs=[SMEM] + [WHOLE] * 8,
        out_specs=WHOLE,
        out_shape=jax.ShapeDtypeStruct(tokens.shape, BF16),
        compiler_params=PARAMS,
        cost_estimate=COST,
        name="finish",
    )(place, tokens, mine, got, last, *routed)


def swap(xs):
    return [xs[0]] + [lax.ppermute(x, "tensor", perm) for x, perm in zip(xs[1:], (NEXT, CORE, FAR))]


def spread(x, near):
    other = lax.ppermute(x, "tensor", CORE)
    far = lax.ppermute(near, "tensor", CORE)
    return x, near, other, far


def fold(mine, others):
    got = lax.ppermute(others, "tensor", CORE)
    rest = (mine[1].astype(F32) + got[1].astype(F32)).astype(BF16)
    return got, lax.ppermute(rest, "tensor", NEXT)


def expert_at(x, z, y):
    return (x * N_Z + z) * N_Y + y


def gather_dense(dense_up, dense_down, before, after):
    rows, units = dense_up.shape
    places = [(x, z, y) for x in range(N_X) for z in range(N_Z) for y in range(N_Y)]
    both = jnp.concatenate([dense_up, dense_down.T], axis=0)
    both, _ = lax.optimization_barrier((both, before))
    mate = lax.ppermute(both, "expert", [(expert_at(x, z, y), expert_at(1 - x, z, y)) for x, z, y in places])
    mate, _ = lax.optimization_barrier((mate, after))
    low = lax.axis_index("expert") < N_Z * N_Y
    pair = jnp.concatenate([jnp.where(low, both, mate), jnp.where(low, mate, both)])
    planes = [[expert_at(x, z, y) for z in range(N_Z) for y in range(N_Y)] for x in range(N_X)]
    out = lax.all_gather(pair, "expert", axis=0, tiled=True, axis_index_groups=planes)
    return out.reshape(N_Z, N_Y, N_X, 2, rows, units)


def local(tokens, expert_ids, gate_codes, dense_up, dense_down, expert_in, expert_out):
    rows_own, width = tokens.shape
    place = lax.axis_index("tensor")
    spot = place.reshape(1)
    n_tensor = lax.axis_size("tensor")
    group = rows_own * n_tensor
    n_experts = lax.axis_size("expert") * expert_in.shape[0]
    capacity = 5 * group // (2 * n_experts)
    part = width // n_tensor

    grouped = swap(pack(spot, tokens, jnp.concatenate([expert_ids.T, gate_codes.T], axis=0)))
    routed, plan = dispatch(spot, grouped, n_experts, capacity)
    weights = gather_dense(dense_up, dense_down, grouped, plan)

    later, _ = lax.optimization_barrier((tokens, grouped))
    tokens_pair = pair_up(tokens, lax.ppermute(later, "tensor", NEXT))

    routed = lax.all_to_all(routed, "expert", split_axis=0, concat_axis=0, tiled=True)
    tokens_by = tokens_pair, lax.ppermute(tokens_pair, "tensor", CORE)
    routed, tokens_by = lax.optimization_barrier((routed, tokens_by))
    start, terms, near, last = 0, [], None, None
    for size in SIZES:
        x = routed[start : start + size]
        start += size
        if near is not None:
            x, near = lax.optimization_barrier((x, near))
        near = lax.ppermute(x, "tensor", NEXT)
        own, beside, other, far = experts(spot, spread(x, near), expert_in[0], expert_out[0], capacity)
        if terms:
            near, own = lax.optimization_barrier((near, own))
        far = lax.ppermute(far, "tensor", CORE)
        other = lax.ppermute(other, "tensor", CORE)
        if terms:
            far, last = lax.optimization_barrier((far, last))
            terms[-1][-1] = last
        rest = (beside.astype(F32) + far.astype(F32)).astype(BF16)
        last = lax.ppermute(rest, "tensor", NEXT)
        terms.append([own, other, last])
    a, b, c = terms[0]
    result = total_of((a.astype(F32) + b.astype(F32) + c.astype(F32)).astype(BF16), terms[1])

    tokens_by, result = lax.optimization_barrier((tokens_by, result))
    mine, others = dense(tokens_by, weights)
    got, last = fold(mine, others)

    returned = lax.all_to_all(result, "expert", split_axis=0, concat_axis=0, tiled=True)
    pieces = swap(combine(spot, returned, plan, capacity))
    return finish(spot, tokens, mine, got, last, pieces)


def solution(mesh):
    return jax.shard_map(
        local,
        mesh=mesh,
        in_specs=(
            P(("expert", "tensor"), None),
            P(("expert", "tensor"), None),
            P(("expert", "tensor"), None),
            P("expert", "tensor"),
            P("tensor", "expert"),
            P("expert", None, "tensor"),
            P("expert", "tensor", None),
        ),
        out_specs=P(("expert", "tensor"), None),
        check_vma=False,
    )
```
